256 devices in a mesh: seq: 64 (over x, y, z_hi, core), head: 4 (over z_lo).
Axes of the slice: x: 4, y: 4, z: 8 (z_hi: 2, z_lo: 4; z = z_hi * 4 + z_lo), core: 2. Of those that a mesh axis runs over, the one named last changes fastest.
Arguments:
- queries: bfloat16 [65536, 2048], P('seq', 'head')
- key_rows: bfloat16 [65536, 2048], P('seq', 'head')
- value_rows: bfloat16 [65536, 2048], P('seq', 'head')
- head_offsets: int32 [16], P('head'), may hold values from 0 to 15, as said below
Outputs:
- attended: bfloat16 [65536, 2048], P('seq', 'head')
The draws below stay inside these ranges and needn't reach their ends.
Inputs may be any that keep to these rules, and one draw needn't show every extreme that they name: `head_offsets`: 1 head share each offset.
All inputs are finite; a program needn't handle non-finite values.
Results may differ from the reference program's by a relative error of at most 0.0034.
Values may be sent and summed in bfloat16 or wider, within the bound.
No kernel may reach another device: no remote copies, remote signals or barrier semaphores. Data moves between devices by JAX's collectives and lax.ppermute only.
A program may use at most 64 MiB of HBM per device.

```python
import jax
import jax.numpy as jnp
from jax import lax

HEADS = 16
DH = 128
W0 = 256
R1 = 4
R2 = 16
TOKENS = 65536
SEG1 = 4096


def log_scales(key, lower, upper):
    return jnp.exp(jax.random.uniform(key, (TOKENS, 1), jnp.float32, jnp.log(lower), jnp.log(upper)))


def draw_queries(key, part):
    key = jax.random.fold_in(key, 11)
    base = 2.0 * jax.random.normal(key, (TOKENS, HEADS * DH), jnp.float32)
    return jnp.clip(base, -16.0, 16.0).astype(jnp.bfloat16)


def draw_key_rows(key, part):
    key = jax.random.fold_in(key, 12)
    base = jax.random.normal(key, (TOKENS, HEADS * DH), jnp.float32)
    return jnp.clip(base, -16.0, 16.0).astype(jnp.bfloat16)


def draw_value_rows(key, part):
    key = jax.random.fold_in(key, 13)
    scale_key, entry_key = jax.random.split(key, 2)
    scales = log_scales(scale_key, 0.3, 3.0)
    base = jax.random.normal(entry_key, (TOKENS, HEADS * DH), jnp.float32)
    return jnp.clip(scales * base, -16.0, 16.0).astype(jnp.bfloat16)


def draw_head_offsets(key, part):
    key = jax.random.fold_in(key, 14)
    return (jax.random.permutation(key, HEADS) % R2).astype(jnp.int32)


def setup_inputs(seed: int = 0) -> dict:
    splits = jax.random.split(jax.random.key(seed), 5)
    queries = draw_queries(jax.random.fold_in(splits[4], 71), 0)
    key_rows = draw_key_rows(jax.random.fold_in(splits[4], 71), 0)
    value_rows = draw_value_rows(jax.random.fold_in(splits[4], 71), 0)
    head_offsets = draw_head_offsets(jax.random.fold_in(splits[4], 71), 0)
    return {"queries": queries, "key_rows": key_rows, "value_rows": value_rows, "head_offsets": head_offsets}


def attend(query_set, key_set, value_set, allowed):
    scaling = query_set.shape[-1] ** -0.5
    scores = jnp.einsum("...qd,...kd->...qk", query_set, key_set) * scaling
    if allowed is not None:
        scores = jnp.where(allowed, scores, -jnp.inf)
    row_max = jnp.max(scores, axis=-1, keepdims=True)
    exponent = jnp.exp(scores - row_max)
    exp_sum = jnp.sum(exponent, axis=-1)
    rounded = lax.optimization_barrier(exponent.astype(jnp.bfloat16))
    weighted = jnp.einsum("...qk,...kd->...qd", rounded.astype(jnp.float32), value_set)
    return weighted / exp_sum[..., None], row_max[..., 0] + jnp.log(exp_sum)


def select_rows(source, stride, which):
    return lax.dynamic_index_in_dim(source.reshape(-1, stride, DH), which, axis=1, keepdims=False)


def spread_rows(rows, stride, which, filler):
    chosen = jnp.arange(stride) == which
    if rows.ndim == 2:
        return jnp.where(chosen[None, :, None], rows[:, None, :], filler).reshape(-1, DH)
    return jnp.where(chosen[None, :], rows[:, None], filler).reshape(-1)


def one_head(head_index, queries, key_rows, value_rows, head_offsets):
    start = head_index * DH
    query_h = lax.dynamic_slice_in_dim(queries, start, DH, axis=1).astype(jnp.float32)
    key_h = lax.dynamic_slice_in_dim(key_rows, start, DH, axis=1).astype(jnp.float32)
    value_h = lax.dynamic_slice_in_dim(value_rows, start, DH, axis=1).astype(jnp.float32)
    head_shift = head_offsets[head_index]
    blocks = TOKENS // W0
    zero_rows = jnp.zeros((W0, DH), jnp.float32)
    prev_keys = jnp.concatenate([zero_rows, key_h[:TOKENS - W0]], 0).reshape(blocks, W0, DH)
    prev_values = jnp.concatenate([zero_rows, value_h[:TOKENS - W0]], 0).reshape(blocks, W0, DH)
    window_keys = jnp.concatenate([prev_keys, key_h.reshape(blocks, W0, DH)], 1)
    window_values = jnp.concatenate([prev_values, value_h.reshape(blocks, W0, DH)], 1)
    barred = (jnp.arange(blocks)[:, None, None] == 0) & (jnp.arange(2 * W0)[None, None, :] < W0)
    local_mix, local_lse = attend(query_h.reshape(blocks, W0, DH), window_keys, window_values, jnp.logical_not(barred))
    local_mix = local_mix.reshape(TOKENS, DH)
    local_lse = local_lse.reshape(TOKENS)

    near_shift = head_shift % R1
    segments = TOKENS // SEG1
    near_q = select_rows(query_h, R1, near_shift).reshape(segments, SEG1 // R1, DH)
    near_k = select_rows(key_h, R1, near_shift).reshape(segments, SEG1 // R1, DH)
    near_v = select_rows(value_h, R1, near_shift).reshape(segments, SEG1 // R1, DH)
    near_mix, near_lse = attend(near_q, near_k, near_v, None)
    near_mix = spread_rows(near_mix.reshape(-1, DH), R1, near_shift, 0.0)
    near_lse = spread_rows(near_lse.reshape(-1), R1, near_shift, -jnp.inf)

    far_q = select_rows(query_h, R2, head_shift)
    far_k = select_rows(key_h, R2, head_shift)
    far_v = select_rows(value_h, R2, head_shift)
    far_mix, far_lse = attend(far_q, far_k, far_v, None)
    far_mix = spread_rows(far_mix, R2, head_shift, 0.0)
    far_lse = spread_rows(far_lse, R2, head_shift, -jnp.inf)

    row_max = jnp.maximum(jnp.maximum(local_lse, near_lse), far_lse)
    local_w = jnp.exp(local_lse - row_max)
    near_w = jnp.exp(near_lse - row_max)
    far_w = jnp.exp(far_lse - row_max)
    merged = (local_w[:, None] * local_mix + near_w[:, None] * near_mix + far_w[:, None] * far_mix) / (local_w + near_w + far_w)[:, None]
    return merged.astype(jnp.bfloat16)


def reference(queries, key_rows, value_rows, head_offsets):
    def per_head(head_index):
        return one_head(head_index, queries, key_rows, value_rows, head_offsets)

    stacked = lax.map(per_head, jnp.arange(HEADS, dtype=jnp.int32))
    return jnp.transpose(stacked, (1, 0, 2)).reshape(TOKENS, HEADS * DH)
```

```python
import functools

import jax
import jax.numpy as jnp
from jax import lax
from jax.experimental import pallas as pl
from jax.experimental.pallas import tpu as pltpu
from jax.sharding import PartitionSpec as P

HEADS = 4
DH = 128
W0 = 256
BLOCKS = 4
TOK = 1024
COLS = 512
NEAR = 64
FAR = 16
SCALE2 = 128**-0.5 * 1.4426950408889634
F32 = jnp.float32
BF16 = jnp.bfloat16

VMEM = pl.BlockSpec(memory_space=pltpu.VMEM)
SMEM = pl.BlockSpec(memory_space=pltpu.SMEM)


def source_row(index, offset):
    order = index >> 4
    residue = ((order & 3) << 2) | (order >> 2)
    return ((index & 15) << 4) + ((offset + residue) & 15)


def select_matrix(offset, count):
    index = lax.broadcasted_iota(jnp.int32, (count, W0), 0)
    row = lax.broadcasted_iota(jnp.int32, (count, W0), 1)
    return jnp.where(row == source_row(index, offset), 1.0, 0.0).astype(BF16)


def restore_matrix(offset):
    index = lax.broadcasted_iota(jnp.int32, (W0, W0), 1)
    row = lax.broadcasted_iota(jnp.int32, (W0, W0), 0)
    return jnp.where(row == source_row(index, offset), 1.0, 0.0).astype(BF16)


def dot(a, b):
    return jnp.dot(a, b, preferred_element_type=F32)


def dot_nt(a, b):
    return lax.dot_general(a, b, (((1,), (1,)), ((), ())), preferred_element_type=F32)


def attend(q, k, v):
    s = dot_nt(q, k) * SCALE2
    m = jnp.max(s, axis=1, keepdims=True)
    p = jnp.exp2(s - m)
    l = jnp.sum(p, axis=1, keepdims=True)
    return m, l, dot(p.astype(BF16), v)


def merge(states):
    m = functools.reduce(jnp.maximum, [s[0] for s in states])
    scales = [jnp.exp2(s[0] - m) for s in states]
    l = sum(s[1] * c for s, c in zip(states, scales))
    acc = sum(s[2] * c for s, c in zip(states, scales))
    return m, l, acc


def head_cols(h):
    return slice(h * DH, (h + 1) * DH)


def value_cols(h):
    return slice(COLS + h * DH, COLS + (h + 1) * DH)


def extract_kernel(off, q, k, v, kv_far, kv_rest, pack, q_near, q_far):
    rest = NEAR - FAR
    for h in range(HEADS):
        sel = select_matrix(off[h], NEAR)
        c, d = head_cols(h), value_cols(h)
        for b in range(BLOCKS):
            rows = slice(b * W0, (b + 1) * W0)
            picked = dot(sel, jnp.concatenate([k[rows, c], v[rows, c]], 1)).astype(BF16)
            f, r = slice(b * FAR, (b + 1) * FAR), slice(b * rest, (b + 1) * rest)
            g = slice(NEAR + b * rest, NEAR + (b + 1) * rest)
            kv_far[f, c] = picked[:FAR, :DH]
            kv_far[f, d] = picked[:FAR, DH:]
            kv_rest[r, c] = picked[FAR:, :DH]
            kv_rest[r, d] = picked[FAR:, DH:]
            pack[f, c] = picked[:FAR, :DH]
            pack[f, d] = picked[:FAR, DH:]
            pack[g, c] = picked[FAR:, :DH]
            pack[g, d] = picked[FAR:, DH:]
        for b in range(0, BLOCKS, 2):
            pair = jnp.concatenate(
                [q[b * W0 : (b + 1) * W0, c], q[(b + 1) * W0 : (b + 2) * W0, c]], 1
            )
            picked = dot(sel, pair).astype(BF16)
            for i in range(2):
                part = picked[:, i * DH : (i + 1) * DH]
                q_near[(b + i) * NEAR : (b + i + 1) * NEAR, c] = part
                q_far[(b + i) * FAR : (b + i + 1) * FAR, c] = part[:FAR]
    pack[W0:, :COLS] = k[TOK - W0 :, :]
    pack[W0:, COLS:] = v[TOK - W0 :, :]


def extract(off, q, k, v):
    return pl.pallas_call(
        extract_kernel,
        out_shape=[
            jax.ShapeDtypeStruct((FAR * BLOCKS, 2 * COLS), BF16),
            jax.ShapeDtypeStruct(((NEAR - FAR) * BLOCKS, 2 * COLS), BF16),
            jax.ShapeDtypeStruct((2 * W0, 2 * COLS), BF16),
            jax.ShapeDtypeStruct((NEAR * BLOCKS, COLS), BF16),
            jax.ShapeDtypeStruct((FAR * BLOCKS, COLS), BF16),
        ],
        in_specs=[SMEM, VMEM, VMEM, VMEM],
        out_specs=[VMEM] * 5,
        compiler_params=pltpu.CompilerParams(vmem_limit_bytes=40 << 20),
        cost_estimate=pl.CostEstimate(
            flops=400_000_000, bytes_accessed=6_000_000, transcendentals=0
        ),
        name="extract",
    )(off, q, k, v)


def local_kernel(off, q, k, v, acc, ml):
    for h in range(HEADS):
        perm = select_matrix(off[h], W0)
        c = head_cols(h)
        for b in range(BLOCKS):
            rows = slice(b * W0, (b + 1) * W0)
            keys = slice(max(b - 1, 0) * W0, (b + 1) * W0)
            qp = dot(perm, q[rows, c]).astype(BF16)
            m, l, o = attend(qp, k[keys, c], v[keys, c])
            acc[rows, c] = o
            ml[rows, h : h + 1] = m
            ml[rows, HEADS + h : HEADS + h + 1] = l


def local(off, q, k, v):
    return pl.pallas_call(
        local_kernel,
        out_shape=[
            jax.ShapeDtypeStruct((TOK, COLS), F32),
            jax.ShapeDtypeStruct((TOK, DH), F32),
        ],
        in_specs=[SMEM, VMEM, VMEM, VMEM],
        out_specs=[VMEM] * 2,
        compiler_params=pltpu.CompilerParams(vmem_limit_bytes=40 << 20),
        cost_estimate=pl.CostEstimate(
            flops=2_000_000_000, bytes_accessed=6_000_000, transcendentals=2_000_000
        ),
        name="local",
    )(off, q, k, v)


def near_kernel(q, far, rest, pack, far_z, far_zc, acc, ml):
    for h in range(HEADS):
        c, d = head_cols(h), value_cols(h)
        k = jnp.concatenate([far[:, c], rest[:, c], pack[:W0, c], far_z[:, c], far_zc[FAR * BLOCKS :, c]], 0)
        v = jnp.concatenate([far[:, d], rest[:, d], pack[:W0, d], far_z[:, d], far_zc[FAR * BLOCKS :, d]], 0)
        m, l, o = attend(q[:, c], k, v)
        acc[:, c] = o
        ml[:, h : h + 1] = m
        ml[:, HEADS + h : HEADS + h + 1] = l


def near(*args):
    return pl.pallas_call(
        near_kernel,
        out_shape=[
            jax.ShapeDtypeStruct((NEAR * BLOCKS, COLS), F32),
            jax.ShapeDtypeStruct((NEAR * BLOCKS, DH), F32),
        ],
        in_specs=[VMEM] * 6,
        out_specs=[VMEM] * 2,
        compiler_params=pltpu.CompilerParams(vmem_limit_bytes=40 << 20),
        cost_estimate=pl.CostEstimate(
            flops=600_000_000, bytes_accessed=3_000_000, transcendentals=600_000
        ),
        name="near",
    )(*args)


def far_kernel(*refs):
    q, kv, out = refs[:4], refs[4:12], refs[12:]
    n = FAR * BLOCKS
    for part in out:
        part[:, COLS:] = jnp.zeros((n, DH), BF16)
    for h in range(HEADS):
        c, d = head_cols(h), value_cols(h)
        qh = jnp.concatenate([x[:, c] for x in q], 0)
        k = jnp.concatenate([x[:, c] for x in kv], 0)
        v = jnp.concatenate([x[:, d] for x in kv], 0)
        m, l, o = attend(qh, k, v)
        o = (o / l).astype(BF16)
        lse = m + jnp.log2(l)
        first = lse.astype(BF16)
        left = lse - first.astype(F32)
        second = left.astype(BF16)
        third = (left - second.astype(F32)).astype(BF16)
        for i, part in enumerate(out):
            rows = slice(i * n, (i + 1) * n)
            part[:, c] = o[rows]
            for e, piece in enumerate((first, second, third)):
                col = COLS + e * HEADS + h
                part[:, col : col + 1] = piece[rows]


def far(*args):
    return pl.pallas_call(
        far_kernel,
        out_shape=[jax.ShapeDtypeStruct((FAR * BLOCKS, COLS + DH), BF16)] * 4,
        in_specs=[VMEM] * 12,
        out_specs=[VMEM] * 4,
        compiler_params=pltpu.CompilerParams(vmem_limit_bytes=40 << 20),
        cost_estimate=pl.CostEstimate(
            flops=1_000_000_000, bytes_accessed=3_000_000, transcendentals=1_000_000
        ),
        name="far",
    )(*args)


def final_kernel(
    off, where, q, acc0, ml0, q_near, acc1, ml1, rest_z, rest_zc, pack, halo, f0, f1, f2, f3, out
):
    from_core = where[0] == 1
    has_halo = where[1] == 1
    for h in range(HEADS):
        c, d = head_cols(h), value_cols(h)
        lc = slice(HEADS + h, HEADS + h + 1)
        mc = slice(h, h + 1)
        k = jnp.concatenate([rest_z[:, c], rest_zc[:, c]], 0)
        v = jnp.concatenate([rest_z[:, d], rest_zc[:, d]], 0)
        near_state = merge([(ml1[:, mc], ml1[:, lc], acc1[:, c]), attend(q_near[:, c], k, v)])
        restore = restore_matrix(off[h])
        for b in range(BLOCKS):
            rows = slice(b * W0, (b + 1) * W0)
            m, l, acc = ml0[rows, mc], ml0[rows, lc], acc0[rows, c]
            if b == 0:
                hk = jnp.where(from_core, pack[W0:, c], halo[:, c])
                hv = jnp.where(from_core, pack[W0:, d], halo[:, d])
                qp = dot(select_matrix(off[h], W0), q[rows, c]).astype(BF16)
                s = jnp.where(has_halo, dot_nt(qp, hk) * SCALE2, -jnp.inf)
                m_new = jnp.maximum(m, jnp.max(s, axis=1, keepdims=True))
                p = jnp.exp2(s - m_new)
                scale = jnp.exp2(m - m_new)
                l = l * scale + jnp.sum(p, axis=1, keepdims=True)
                acc = acc * scale + dot(p.astype(BF16), hv)
                m = m_new
            near_rows = slice(b * NEAR, (b + 1) * NEAR)
            far_rows = slice(b * FAR, (b + 1) * FAR)
            m1, l1, a1 = merge(
                [(m[:NEAR], l[:NEAR], acc[:NEAR]), tuple(x[near_rows] for x in near_state)]
            )
            parts = [(m1[:FAR], l1[:FAR], a1[:FAR])]
            for f in (f0, f1, f2, f3):
                lse = sum(
                    f[far_rows, COLS + e * HEADS + h : COLS + e * HEADS + h + 1].astype(F32)
                    for e in range(3)
                )
                parts.append((lse, jnp.ones_like(lse), f[far_rows, c].astype(F32)))
            m2, l2, a2 = merge(parts)
            mixed = jnp.concatenate(
                [a2 / l2, a1[FAR:] / l1[FAR:], acc[NEAR:] / l[NEAR:]], 0
            ).astype(BF16)
            out[rows, c] = dot(restore, mixed).astype(BF16)


def final(*args):
    return pl.pallas_call(
        final_kernel,
        out_shape=jax.ShapeDtypeStruct((TOK, COLS), BF16),
        in_specs=[SMEM, SMEM] + [VMEM] * 14,
        out_specs=VMEM,
        compiler_params=pltpu.CompilerParams(vmem_limit_bytes=40 << 20),
        cost_estimate=pl.CostEstimate(
            flops=1_000_000_000, bytes_accessed=6_000_000, transcendentals=1_000_000
        ),
        name="final",
    )(*args)


def place(x, y, z, core):
    return ((x % 4 * 4 + y % 4) * 2 + z % 2) * 2 + core


def moves(dx=0, dy=0, dz=0, dcore=0):
    return [
        (place(x, y, z, core), place(x + dx, y + dy, z + dz, (core + dcore) % 2))
        for x in range(4)
        for y in range(4)
        for z in range(2)
        for core in range(2)
    ]


def send(value, **shift):
    return lax.ppermute(value, "seq", moves(**shift))


def shards(q, k, v, off):
    position = lax.axis_index("seq")
    where = jnp.stack([position & 1, jnp.minimum(position, 1)]).astype(jnp.int32)
    kv_far, kv_rest, pack, q_near, q_far = extract(off, q, k, v)
    pack_c = send(pack, dcore=1)
    far_z = send(kv_far, dz=1)
    rest_z = send(kv_rest, dz=1)
    halo = lax.ppermute(pack[W0:], "seq", [(s, s + 1) for s in range(1, 63, 2)])
    qs = [q_far] + [send(q_far, dy=s) for s in (1, -1, 2)]
    own = jnp.concatenate([kv_far, far_z], 0)
    gathered = [own] + [send(own, dx=s) for s in (1, -1, 2)]
    crossed = [send(x, dcore=1) for x in gathered]
    acc0, ml0 = local(off, q, k, v)
    far_zc = crossed[0]
    acc1, ml1 = near(q_near, kv_far, kv_rest, pack_c, far_z, far_zc)
    parts = far(*qs, *gathered, *crossed)
    back = [parts[0]] + [send(p, dy=-s) for p, s in zip(parts[1:], (1, -1, 2))]
    rest_zc = send(rest_z, dcore=1)
    return final(
        off, where, q, acc0, ml0, q_near, acc1, ml1, rest_z, rest_zc, pack_c, halo, *back
    )


def solution(mesh):
    placed = (P("seq", "head"), P("seq", "head"), P("seq", "head"), P("head"))
    return jax.shard_map(
        shards, mesh=mesh, in_specs=placed, out_specs=P("seq", "head"), check_vma=False
    )
```

```python
import functools

import jax
import jax.numpy as jnp
from jax import lax
from jax.experimental import pallas as pl
from jax.experimental.pallas import tpu as pltpu
from jax.sharding import PartitionSpec as P

HEADS = 4
DH = 128
W0 = 256
BLOCKS = 4
TOK = 1024
COLS = 512
NEAR = 64
FAR = 16
REST = NEAR - FAR
OTHER = W0 - NEAR
NROWS = NEAR * BLOCKS
FROWS = FAR * BLOCKS
KEPT = OTHER + NROWS
SENT = COLS + 3 * DH
SCALE2 = 128**-0.5 * 1.4426950408889634
F32 = jnp.float32
BF16 = jnp.bfloat16

VMEM = pl.BlockSpec(memory_space=pltpu.VMEM)
HBM = pl.BlockSpec(memory_space=pltpu.HBM)


def out_of(*shape, dtype=BF16):
    return jax.ShapeDtypeStruct(shape, dtype)


def params(mib):
    return pltpu.CompilerParams(vmem_limit_bytes=mib << 20)


def cost(us):
    return pl.CostEstimate(flops=int(us * 1e9), bytes_accessed=1000, transcendentals=0)


def source_row(index, offset):
    order = index >> 4
    residue = ((order & 3) << 2) + (((order >> 2) + 1) & 3)
    return ((index & 15) << 4) + ((offset + residue) & 15)


def select_matrix(offset, start, count):
    index = lax.broadcasted_iota(jnp.int32, (count, W0), 0) + start
    row = lax.broadcasted_iota(jnp.int32, (count, W0), 1)
    return jnp.where(row == source_row(index, offset), 1.0, 0.0).astype(BF16)


def restore_matrix(offset, start, count):
    index = lax.broadcasted_iota(jnp.int32, (W0, count), 1) + start
    row = lax.broadcasted_iota(jnp.int32, (W0, count), 0)
    return jnp.where(row == source_row(index, offset), 1.0, 0.0).astype(BF16)


def dot(a, b):
    return jnp.dot(a, b, preferred_element_type=F32)


def dot_nt(a, b):
    return lax.dot_general(a, b, (((1,), (1,)), ((), ())), preferred_element_type=F32)


def wide(column):
    return jnp.broadcast_to(column, (column.shape[0], DH))


def attend(q, k, v):
    s = dot_nt(q, k) * SCALE2
    m = jnp.max(s, axis=1, keepdims=True)
    p = jnp.exp2(s - m)
    l = jnp.sum(p, axis=1, keepdims=True)
    return wide(m), wide(l), dot(p.astype(BF16), v)


def merge(states):
    m = functools.reduce(jnp.maximum, [s[0] for s in states])
    scales = [jnp.exp2(s[0] - m) for s in states]
    l = sum(s[1] * c for s, c in zip(states, scales))
    acc = sum(s[2] * c for s, c in zip(states, scales))
    return m, l, acc


def head_cols(h):
    return slice(h * DH, (h + 1) * DH)


def value_cols(h):
    return slice(COLS + h * DH, COLS + (h + 1) * DH)


def block_rows(b):
    return slice(b * W0, (b + 1) * W0)


def offset_rows(offs, h, width):
    row = offs[h : h + 1, :]
    return jnp.concatenate([row] * (width // DH), 1) if width > DH else row[:, :width]


def extract_kernel(
    off_hbm, k_hbm, v_hbm, offs, kv_far, kv_rest, halo, pack, off, k, v, off_sem, sems
):
    off_copy = pltpu.make_async_copy(off_hbm, off, off_sem)
    off_copy.start()
    copies = {}
    for b in range(BLOCKS):
        for i, (src, dst) in enumerate(((k_hbm, k), (v_hbm, v))):
            copies[i, b] = pltpu.make_async_copy(
                src.at[block_rows(b), :], dst.at[block_rows(b), :], sems.at[i, b]
            )
            copies[i, b].start()
    off_copy.wait()
    sels = []
    for h in range(HEADS):
        offs[h : h + 1, :] = jnp.full((1, DH), off[h], jnp.int32)
        sels.append(select_matrix(off[h], OTHER, NEAR))
    for b in range(BLOCKS):
        rows = block_rows(b)
        copies[0, b].wait()
        copies[1, b].wait()
        f, r = slice(b * FAR, (b + 1) * FAR), slice(b * REST, (b + 1) * REST)
        g = slice(FROWS + b * REST, FROWS + (b + 1) * REST)
        for h in range(HEADS):
            c, d = head_cols(h), value_cols(h)
            picked = dot(sels[h], jnp.concatenate([k[rows, c], v[rows, c]], 1)).astype(BF16)
            for cols, part in ((c, picked[:, :DH]), (d, picked[:, DH:])):
                kv_far[f, cols] = part[:FAR]
                pack[f, cols] = part[:FAR]
                kv_rest[r, cols] = part[FAR:]
                pack[g, cols] = part[FAR:]
    last = block_rows(BLOCKS - 1)
    for out, rows in ((halo, slice(0, W0)), (pack, slice(NROWS, NROWS + W0))):
        out[rows, :COLS] = k[last, :]
        out[rows, COLS:] = v[last, :]


def extract(*args):
    return pl.pallas_call(
        extract_kernel,
        out_shape=[
            out_of(8, DH, dtype=jnp.int32),
            out_of(FROWS, 2 * COLS),
            out_of(REST * BLOCKS, 2 * COLS),
            out_of(W0, 2 * COLS),
            out_of(NROWS + W0, 2 * COLS),
        ],
        in_specs=[HBM] * 3,
        out_specs=[VMEM] * 5,
        scratch_shapes=[
            pltpu.SMEM((HEADS,), jnp.int32),
            pltpu.VMEM((TOK, COLS), BF16),
            pltpu.VMEM((TOK, COLS), BF16),
            pltpu.SemaphoreType.DMA,
            pltpu.SemaphoreType.DMA((2, BLOCKS)),
        ],
        compiler_params=params(59),
        cost_estimate=cost(0),
        name="extract",
    )(*args)


def queries_kernel(offs, q_hbm, qp, qn, qf, res, q, sems):
    copies = []
    for b in range(BLOCKS):
        copies.append(
            pltpu.make_async_copy(q_hbm.at[block_rows(b), :], q.at[block_rows(b), :], sems.at[b])
        )
        copies[-1].start()
    sels = []
    for h in range(HEADS):
        offset = offset_rows(offs, h, W0)
        sels.append(select_matrix(offset, 0, W0))
        res[block_rows(h), :] = restore_matrix(offset, 0, W0)
    for b in range(0, BLOCKS, 2):
        copies[b].wait()
        copies[b + 1].wait()
        for h in range(HEADS):
            c = head_cols(h)
            pair = jnp.concatenate([q[block_rows(b), c], q[block_rows(b + 1), c]], 1)
            moved = dot(sels[h], pair).astype(BF16)
            for i in range(2):
                part = moved[:, i * DH : (i + 1) * DH]
                qp[block_rows(b + i), c] = part
                qn[(b + i) * NEAR : (b + i + 1) * NEAR, c] = part[OTHER:]
                qf[(b + i) * FAR : (b + i + 1) * FAR, c] = part[OTHER : OTHER + FAR]


def permute_queries(*args):
    return pl.pallas_call(
        queries_kernel,
        out_shape=[
            out_of(TOK, COLS),
            out_of(NROWS, COLS),
            out_of(FROWS, COLS),
            out_of(HEADS * W0, W0),
        ],
        in_specs=[VMEM, HBM],
        out_specs=[VMEM] * 4,
        scratch_shapes=[pltpu.VMEM((TOK, COLS), BF16), pltpu.SemaphoreType.DMA((BLOCKS,))],
        compiler_params=params(16),
        cost_estimate=cost(3),
        name="queries",
    )(*args)


def own_kernel(kv_far, far_z, own):
    own[:FROWS, :] = kv_far[...]
    own[FROWS:, :] = far_z[...]


def join_far(*args):
    return pl.pallas_call(
        own_kernel,
        out_shape=out_of(2 * FROWS, 2 * COLS),
        in_specs=[VMEM] * 2,
        out_specs=VMEM,
        compiler_params=params(8),
        cost_estimate=cost(0),
        name="own",
    )(*args)


def local_kernel(res, q, k, v, done, km, kl, ka):
    for h in range(HEADS):
        c = head_cols(h)
        qs = [q[block_rows(b), c] for b in range(BLOCKS)]
        scores = [[] for _ in range(BLOCKS)]
        for j in range(BLOCKS):
            users = qs[j : j + 2]
            s = dot_nt(jnp.concatenate(users, 0), k[block_rows(j), c]) * SCALE2
            for i in range(len(users)):
                scores[j + i].append(s[i * W0 : (i + 1) * W0])
        ms, ls, ps = [], [], []
        for b in range(BLOCKS):
            m = functools.reduce(
                jnp.maximum, [jnp.max(s, axis=1, keepdims=True) for s in scores[b]]
            )
            p = [jnp.exp2(s - m) for s in scores[b]]
            ms.append(m)
            ls.append(sum(jnp.sum(x, axis=1, keepdims=True) for x in p))
            ps.append([x.astype(BF16) for x in p])
        accs = [None] * BLOCKS
        for j in range(BLOCKS):
            users = [ps[j][-1]] + ([ps[j + 1][0]] if j + 1 < BLOCKS else [])
            o = dot(jnp.concatenate(users, 0), v[block_rows(j), c])
            for i in range(len(users)):
                part = o[i * W0 : (i + 1) * W0]
                accs[j + i] = part if accs[j + i] is None else accs[j + i] + part
        km[:W0, c], kl[:W0, c], ka[:W0, c] = wide(ms[0]), wide(ls[0]), accs[0]
        rest = []
        for b in range(1, BLOCKS):
            near = slice(OTHER + b * NEAR, OTHER + (b + 1) * NEAR)
            km[near, c] = wide(ms[b][OTHER:])
            kl[near, c] = wide(ls[b][OTHER:])
            ka[near, c] = accs[b][OTHER:]
            rest.append((accs[b][:OTHER] * (1.0 / ls[b][:OTHER])).astype(BF16))
        restore = res[block_rows(h), :OTHER]
        pair = dot(restore, jnp.concatenate(rest[:2], 1)).astype(BF16)
        done[0:W0, c] = pair[:, :DH]
        done[W0 : 2 * W0, c] = pair[:, DH:]
        done[2 * W0 :, c] = dot(restore, rest[2]).astype(BF16)


def local(*args):
    state = out_of(KEPT, COLS, dtype=F32)
    return pl.pallas_call(
        local_kernel,
        out_shape=[
            out_of(TOK - W0, COLS),
            state,
            state,
            state,
        ],
        in_specs=[VMEM] * 4,
        out_specs=[VMEM] * 4,
        compiler_params=params(16),
        cost_estimate=cost(1),
        name="local",
    )(*args)


def halo_kernel(res, q, km, kl, ka, pack, halo, done, hm, hl, ha):
    position = lax.axis_index("seq")
    from_core = (position & 1) == 1
    has_halo = position > 0
    for h in range(HEADS):
        c, d = head_cols(h), value_cols(h)
        hk = jnp.where(from_core, pack[NROWS:, c], halo[:, c])
        hv = jnp.where(from_core, pack[NROWS:, d], halo[:, d])
        m = km[:W0, c]
        s = jnp.where(has_halo, dot_nt(q[:W0, c], hk) * SCALE2, -jnp.inf)
        m_new = jnp.maximum(m, wide(jnp.max(s, axis=1, keepdims=True)))
        p = jnp.exp2(s - jnp.concatenate([m_new, m_new], 1))
        scale = jnp.exp2(m - m_new)
        l = kl[:W0, c] * scale + wide(jnp.sum(p, axis=1, keepdims=True))
        acc = ka[:W0, c] * scale + dot(p.astype(BF16), hv)
        hm[:, c], hl[:, c], ha[:, c] = m_new[OTHER:], l[OTHER:], acc[OTHER:]
        rest = (acc[:OTHER] * (1.0 / l[:OTHER])).astype(BF16)
        done[:, c] = dot(res[block_rows(h), :OTHER], rest).astype(BF16)


def halo_fold(*args):
    state = out_of(NEAR, COLS, dtype=F32)
    return pl.pallas_call(
        halo_kernel,
        out_shape=[out_of(W0, COLS), state, state, state],
        in_specs=[VMEM] * 7,
        out_specs=[VMEM] * 4,
        compiler_params=params(16),
        cost_estimate=cost(0),
        name="halo",
    )(*args)


def near_kernel(q, far, rest, pack, m, l, acc):
    for h in range(HEADS):
        c, d = head_cols(h), value_cols(h)
        k, v = (
            jnp.concatenate([far[:, cols], rest[:, cols], pack[:NROWS, cols]], 0)
            for cols in (c, d)
        )
        m[:, c], l[:, c], acc[:, c] = attend(q[:, c], k, v)


def near(*args):
    return pl.pallas_call(
        near_kernel,
        out_shape=[out_of(NROWS, COLS, dtype=F32)] * 3,
        in_specs=[VMEM] * 4,
        out_specs=[VMEM] * 3,
        compiler_params=params(16),
        cost_estimate=cost(0),
        name="near",
    )(*args)


def far_kernel(*refs):
    q, kv, out = refs[:4], refs[4:12], refs[12:]
    for part in out:
        part[:, COLS:] = jnp.zeros((FROWS, 3 * DH), BF16)
    for h in range(HEADS):
        c, d = head_cols(h), value_cols(h)
        qh = jnp.concatenate([x[:, c] for x in q], 0)
        k = jnp.concatenate([x[:, c] for x in kv], 0)
        v = jnp.concatenate([x[:, d] for x in kv], 0)
        m, l, o = attend(qh, k, v)
        o = (o * (1.0 / l)).astype(BF16)
        lse = (m + jnp.log2(l))[:, :1]
        first = lse.astype(BF16)
        left = lse - first.astype(F32)
        second = left.astype(BF16)
        third = (left - second.astype(F32)).astype(BF16)
        for i, part in enumerate(out):
            rows = slice(i * FROWS, (i + 1) * FROWS)
            part[:, c] = o[rows]
            for e, piece in enumerate((first, second, third)):
                col = COLS + e * DH + h
                part[:, col : col + 1] = piece[rows]


def far(*args):
    return pl.pallas_call(
        far_kernel,
        out_shape=[out_of(FROWS, SENT)] * 4,
        in_specs=[VMEM] * 12,
        out_specs=[VMEM] * 4,
        compiler_params=params(16),
        cost_estimate=cost(0),
        name="far",
    )(*args)


def join_kernel(
    far_z, res, q, km, kl, ka, hm, hl, ha, nm, nl, na, far_zc, rest_z, rest_zc, done0, done, f0, f1, f2, f3, out
):
    fars = (f0, f1, f2, f3)
    lses = [
        sum(f[:, COLS + e * DH : COLS + (e + 1) * DH].astype(F32) for e in range(3)) for f in fars
    ]
    for h in range(HEADS):
        c, d = head_cols(h), value_cols(h)
        k, v = (
            jnp.concatenate(
                [far_z[:, cols], far_zc[FROWS:, cols], rest_z[:, cols], rest_zc[:, cols]], 0
            )
            for cols in (c, d)
        )
        state = tuple(
            jnp.concatenate([x[:, c], y[W0:, c]], 0) for x, y in ((hm, km), (hl, kl), (ha, ka))
        )
        m, l, acc = merge([state, (nm[:, c], nl[:, c], na[:, c]), attend(q[:, c], k, v)])
        parts = [(wide(x[:, h : h + 1]), f[:, c].astype(F32)) for x, f in zip(lses, fars)]
        restored = []
        for b in range(BLOCKS):
            rows = slice(b * NEAR, (b + 1) * NEAR)
            mb, lb, ab = m[rows], l[rows], acc[rows]
            fr = slice(b * FAR, (b + 1) * FAR)
            _, lf, af = merge(
                [(mb[:FAR], lb[:FAR], ab[:FAR])] + [(x[fr], 1.0, o[fr]) for x, o in parts]
            )
            restored.append(
                (
                    jnp.concatenate([af, ab[FAR:]], 0)
                    * (1.0 / jnp.concatenate([lf, lb[FAR:]], 0))
                ).astype(BF16)
            )
        placed = dot(res[block_rows(h), OTHER:], jnp.concatenate(restored, 1)).astype(BF16)
        out[:W0, c] = done0[:, c] + placed[:, :DH]
        for b in range(1, BLOCKS):
            rows = slice((b - 1) * W0, b * W0)
            out[block_rows(b), c] = done[rows, c] + placed[:, b * DH : (b + 1) * DH]


def join(*args):
    return pl.pallas_call(
        join_kernel,
        out_shape=out_of(TOK, COLS),
        in_specs=[VMEM] * 21,
        out_specs=VMEM,
        compiler_params=params(16),
        cost_estimate=cost(0),
        name="join",
    )(*args)


def place(x, y, z, core):
    return ((x % 4 * 4 + y % 4) * 2 + z % 2) * 2 + core


def moves(dx=0, dy=0, dz=0, dcore=0):
    return [
        (place(x, y, z, core), place(x + dx, y + dy, z + dz, (core + dcore) % 2))
        for x in range(4)
        for y in range(4)
        for z in range(2)
        for core in range(2)
    ]


def send(value, **shift):
    return lax.ppermute(value, "seq", moves(**shift))


def shards(q, k, v, off):
    offs, kv_far, kv_rest, halo, pack = extract(off, k, v)
    far_z = send(kv_far, dz=1)
    pack_c = send(pack, dcore=1)
    qp, qn, qf, res = permute_queries(offs, q)
    halo = lax.ppermute(halo, "seq", [(s, s + 1) for s in range(1, 63, 2)])
    qf, pack_c = lax.optimization_barrier((qf, pack_c))
    qs = [send(qf, dy=s) for s in (1, -1, 2)]
    far_z, qs = lax.optimization_barrier((far_z, qs))
    own = join_far(kv_far, far_z)
    own, kv_rest = lax.optimization_barrier((own, kv_rest))
    gathered = [own] + [send(own, dx=s) for s in (1, -1, 2)]
    rest_z = send(kv_rest, dz=1)
    done, km, kl, ka = local(res, qp, k, v)
    near_state = near(qn, kv_far, kv_rest, pack_c)
    done0, *halo_state = halo_fold(res, qp, km, kl, ka, pack_c, halo)
    gathered, near_state, done0 = lax.optimization_barrier((gathered, near_state, done0))
    crossed = [send(x, dcore=1) for x in gathered]
    parts = far(qf, *qs, *gathered, *crossed)
    back = [parts[0]] + [send(p, dy=-s) for p, s in zip(parts[1:], (1, -1, 2))]
    rest_z, *back = lax.optimization_barrier((rest_z, *back))
    rest_zc = send(rest_z, dcore=1)
    return join(
        far_z, res, qn, km, kl, ka, *halo_state, *near_state, crossed[0], rest_z, rest_zc,
        done0, done, *back,
    )


def solution(mesh):
    placed = (P("seq", "head"), P("seq", "head"), P("seq", "head"), P("head"))
    return jax.shard_map(
        shards, mesh=mesh, in_specs=placed, out_specs=P("seq", "head"), check_vma=False
    )
```

```python
import functools

import jax
import jax.numpy as jnp
from jax import lax
from jax.experimental import pallas as pl
from jax.experimental.pallas import tpu as pltpu
from jax.sharding import PartitionSpec as P

HEADS = 4
DH = 128
W0 = 256
BLOCKS = 4
R1 = 4
R2 = 16
TOK = 1024
COLS = 512
NEAR = 64
FAR = 16
REST = NEAR - FAR
OTHER = W0 - NEAR
NROWS = NEAR * BLOCKS
FROWS = FAR * BLOCKS
KEPT = OTHER + NROWS
SENT = COLS + 3 * DH
SCALE2 = 128**-0.5 * 1.4426950408889634
F32 = jnp.float32
BF16 = jnp.bfloat16

VMEM = pl.BlockSpec(memory_space=pltpu.VMEM)
HBM = pl.BlockSpec(memory_space=pltpu.HBM)


def out_of(*shape, dtype=BF16):
    return jax.ShapeDtypeStruct(shape, dtype)


def params(mib):
    return pltpu.CompilerParams(vmem_limit_bytes=mib << 20)


def cost(us):
    return pl.CostEstimate(flops=int(us * 1e9), bytes_accessed=1000, transcendentals=0)


def source_row(index, offset):
    order = index >> 4
    residue = ((order & 3) << 2) + (((order >> 2) + 1) & 3)
    return ((index & 15) << 4) + ((offset + residue) & 15)


def select_matrix(offset, start, count):
    index = lax.broadcasted_iota(jnp.int32, (count, W0), 0) + start
    row = lax.broadcasted_iota(jnp.int32, (count, W0), 1)
    return jnp.where(row == source_row(index, offset), 1.0, 0.0).astype(BF16)


def restore_matrix(offset, start, count):
    index = lax.broadcasted_iota(jnp.int32, (W0, count), 1) + start
    row = lax.broadcasted_iota(jnp.int32, (W0, count), 0)
    return jnp.where(row == source_row(index, offset), 1.0, 0.0).astype(BF16)


def dot(a, b):
    return jnp.dot(a, b, preferred_element_type=F32)


def dot_nt(a, b):
    return lax.dot_general(a, b, (((1,), (1,)), ((), ())), preferred_element_type=F32)


def wide(column):
    return jnp.broadcast_to(column, (column.shape[0], DH))


def attend(q, k, v):
    s = dot_nt(q, k) * SCALE2
    m = jnp.max(s, axis=1, keepdims=True)
    p = jnp.exp2(s - m)
    l = jnp.sum(p, axis=1, keepdims=True)
    return wide(m), wide(l), dot(p.astype(BF16), v)


def merge(states):
    m = functools.reduce(jnp.maximum, [s[0] for s in states])
    scales = [jnp.exp2(s[0] - m) for s in states]
    l = sum(s[1] * c for s, c in zip(states, scales))
    acc = sum(s[2] * c for s, c in zip(states, scales))
    return m, l, acc


def head_cols(h):
    return slice(h * DH, (h + 1) * DH)


def value_cols(h):
    return slice(COLS + h * DH, COLS + (h + 1) * DH)


def block_rows(b):
    return slice(b * W0, (b + 1) * W0)


def offset_rows(offs, h, width):
    row = offs[h : h + 1, :]
    return jnp.concatenate([row] * (width // DH), 1) if width > DH else row[:, :width]


def extract_kernel(
    off_hbm, k_hbm, v_hbm, offs, kv_far, kv_rest, kv_near, halo, off, k, v, k32, v32, off_sem, sems
):
    off_copy = pltpu.make_async_copy(off_hbm, off, off_sem)
    off_copy.start()
    copies = {}
    for b in reversed(range(BLOCKS)):
        for i, (src, dst) in enumerate(((k_hbm, k), (v_hbm, v))):
            copies[i, b] = pltpu.make_async_copy(
                src.at[block_rows(b), :], dst.at[block_rows(b), :], sems.at[i, b]
            )
            copies[i, b].start()
    off_copy.wait()
    for h in range(HEADS):
        offs[h : h + 1, :] = jnp.full((1, DH), off[h], jnp.int32)
    for b in reversed(range(BLOCKS)):
        rows = block_rows(b)
        for i, (src, dst) in enumerate(((k, k32), (v, v32))):
            copies[i, b].wait()
            if b == BLOCKS - 1:
                copies[i, BLOCKS] = pltpu.make_async_copy(
                    src.at[rows, :], halo.at[:, i * COLS : (i + 1) * COLS], sems.at[i, BLOCKS]
                )
                copies[i, BLOCKS].start()
            for h in range(HEADS):
                dst[h, rows, :] = src[rows, head_cols(h)].astype(F32)
    for h in range(HEADS):
        for a in range(R2 // R1):
            start = (off[h] + R1 * a) & (R2 - 1)
            for src, cols in ((k32, head_cols(h)), (v32, value_cols(h))):
                part = src[h, pl.ds(start, FROWS, stride=R2), :].astype(BF16)
                kv_near[a * FROWS : (a + 1) * FROWS, cols] = part
                if a == 0:
                    kv_far[:, cols] = part
                else:
                    kv_rest[(a - 1) * FROWS : a * FROWS, cols] = part
    for i in range(2):
        copies[i, BLOCKS].wait()


def extract(*args):
    return pl.pallas_call(
        extract_kernel,
        out_shape=[
            out_of(8, DH, dtype=jnp.int32),
            out_of(FROWS, 2 * COLS),
            out_of(REST * BLOCKS, 2 * COLS),
            out_of(NROWS, 2 * COLS),
            out_of(W0, 2 * COLS),
        ],
        in_specs=[HBM] * 3,
        out_specs=[VMEM] * 4 + [HBM],
        scratch_shapes=[
            pltpu.SMEM((HEADS,), jnp.int32),
            pltpu.VMEM((TOK, COLS), BF16),
            pltpu.VMEM((TOK, COLS), BF16),
            pltpu.VMEM((HEADS, TOK, DH), F32),
            pltpu.VMEM((HEADS, TOK, DH), F32),
            pltpu.SemaphoreType.DMA,
            pltpu.SemaphoreType.DMA((2, BLOCKS + 1)),
        ],
        compiler_params=params(59),
        cost_estimate=cost(0),
        name="extract",
    )(*args)


def queries_kernel(offs, q_hbm, qp, qn, qf, res, q, sems):
    copies = []
    for b in range(BLOCKS):
        copies.append(
            pltpu.make_async_copy(q_hbm.at[block_rows(b), :], q.at[block_rows(b), :], sems.at[b])
        )
        copies[-1].start()
    sels = []
    for h in range(HEADS):
        offset = offset_rows(offs, h, W0)
        sels.append(select_matrix(offset, 0, W0))
        res[block_rows(h), :] = restore_matrix(offset, 0, W0)
    for b in range(0, BLOCKS, 2):
        copies[b].wait()
        copies[b + 1].wait()
        for h in range(HEADS):
            c = head_cols(h)
            pair = jnp.concatenate([q[block_rows(b), c], q[block_rows(b + 1), c]], 1)
            moved = dot(sels[h], pair).astype(BF16)
            for i in range(2):
                part = moved[:, i * DH : (i + 1) * DH]
                qp[block_rows(b + i), c] = part
                qn[(b + i) * NEAR : (b + i + 1) * NEAR, c] = part[OTHER:]
                qf[(b + i) * FAR : (b + i + 1) * FAR, c] = part[OTHER : OTHER + FAR]


def permute_queries(*args):
    return pl.pallas_call(
        queries_kernel,
        out_shape=[
            out_of(TOK, COLS),
            out_of(NROWS, COLS),
            out_of(FROWS, COLS),
            out_of(HEADS * W0, W0),
        ],
        in_specs=[VMEM, HBM],
        out_specs=[VMEM] * 4,
        scratch_shapes=[pltpu.VMEM((TOK, COLS), BF16), pltpu.SemaphoreType.DMA((BLOCKS,))],
        compiler_params=params(16),
        cost_estimate=cost(12),
        name="queries",
    )(*args)


def own_kernel(kv_far, far_z, own):
    own[:FROWS, :] = kv_far[...]
    own[FROWS:, :] = far_z[...]


def join_far(*args):
    return pl.pallas_call(
        own_kernel,
        out_shape=out_of(2 * FROWS, 2 * COLS),
        in_specs=[VMEM] * 2,
        out_specs=VMEM,
        compiler_params=params(8),
        cost_estimate=cost(0),
        name="own",
    )(*args)


def local_kernel(res, q, k, v, done, km, kl, ka):
    for h in range(HEADS):
        c = head_cols(h)
        qs = [q[block_rows(b), c] for b in range(BLOCKS)]
        scores = [[] for _ in range(BLOCKS)]
        for j in range(BLOCKS):
            users = qs[j : j + 2]
            s = dot_nt(jnp.concatenate(users, 0), k[block_rows(j), c]) * SCALE2
            for i in range(len(users)):
                scores[j + i].append(s[i * W0 : (i + 1) * W0])
        ms, ls, ps = [], [], []
        for b in range(BLOCKS):
            m = functools.reduce(
                jnp.maximum, [jnp.max(s, axis=1, keepdims=True) for s in scores[b]]
            )
            p = [jnp.exp2(s - m) for s in scores[b]]
            ms.append(m)
            ls.append(sum(jnp.sum(x, axis=1, keepdims=True) for x in p))
            ps.append([x.astype(BF16) for x in p])
        accs = [None] * BLOCKS
        for j in range(BLOCKS):
            users = [ps[j][-1]] + ([ps[j + 1][0]] if j + 1 < BLOCKS else [])
            o = dot(jnp.concatenate(users, 0), v[block_rows(j), c])
            for i in range(len(users)):
                part = o[i * W0 : (i + 1) * W0]
                accs[j + i] = part if accs[j + i] is None else accs[j + i] + part
        km[:W0, c], kl[:W0, c], ka[:W0, c] = wide(ms[0]), wide(ls[0]), accs[0]
        rest = []
        for b in range(1, BLOCKS):
            near = slice(OTHER + b * NEAR, OTHER + (b + 1) * NEAR)
            km[near, c] = wide(ms[b][OTHER:])
            kl[near, c] = wide(ls[b][OTHER:])
            ka[near, c] = accs[b][OTHER:]
            rest.append((accs[b][:OTHER] * (1.0 / ls[b][:OTHER])).astype(BF16))
        restore = res[block_rows(h), :OTHER]
        pair = dot(restore, jnp.concatenate(rest[:2], 1)).astype(BF16)
        done[0:W0, c] = pair[:, :DH]
        done[W0 : 2 * W0, c] = pair[:, DH:]
        done[2 * W0 :, c] = dot(restore, rest[2]).astype(BF16)


def local(*args):
    state = out_of(KEPT, COLS, dtype=F32)
    return pl.pallas_call(
        local_kernel,
        out_shape=[
            out_of(TOK - W0, COLS),
            state,
            state,
            state,
        ],
        in_specs=[VMEM] * 4,
        out_specs=[VMEM] * 4,
        compiler_params=params(16),
        cost_estimate=cost(1),
        name="local",
    )(*args)


def halo_kernel(res, q, km, kl, ka, halo_c, halo, done, hm, hl, ha):
    position = lax.axis_index("seq")
    from_core = (position & 1) == 1
    has_halo = position > 0
    for h in range(HEADS):
        c, d = head_cols(h), value_cols(h)
        hk = jnp.where(from_core, halo_c[:, c], halo[:, c])
        hv = jnp.where(from_core, halo_c[:, d], halo[:, d])
        m = km[:W0, c]
        s = jnp.where(has_halo, dot_nt(q[:W0, c], hk) * SCALE2, -jnp.inf)
        m_new = jnp.maximum(m, wide(jnp.max(s, axis=1, keepdims=True)))
        p = jnp.exp2(s - jnp.concatenate([m_new, m_new], 1))
        scale = jnp.exp2(m - m_new)
        l = kl[:W0, c] * scale + wide(jnp.sum(p, axis=1, keepdims=True))
        acc = ka[:W0, c] * scale + dot(p.astype(BF16), hv)
        hm[:, c], hl[:, c], ha[:, c] = m_new[OTHER:], l[OTHER:], acc[OTHER:]
        rest = (acc[:OTHER] * (1.0 / l[:OTHER])).astype(BF16)
        done[:, c] = dot(res[block_rows(h), :OTHER], rest).astype(BF16)


def halo_fold(*args):
    state = out_of(NEAR, COLS, dtype=F32)
    return pl.pallas_call(
        halo_kernel,
        out_shape=[out_of(W0, COLS), state, state, state],
        in_specs=[VMEM] * 7,
        out_specs=[VMEM] * 4,
        compiler_params=params(16),
        cost_estimate=cost(0),
        name="halo",
    )(*args)


def near_kernel(q, km, kl, ka, hm, hl, ha, near, near_c, far_z, m, l, acc):
    for h in range(HEADS):
        c, d = head_cols(h), value_cols(h)
        k, v = (
            jnp.concatenate([near[:, cols], near_c[:, cols], far_z[:, cols]], 0)
            for cols in (c, d)
        )
        state = tuple(
            jnp.concatenate([x[:, c], y[W0:, c]], 0) for x, y in ((hm, km), (hl, kl), (ha, ka))
        )
        m[:, c], l[:, c], acc[:, c] = merge([state, attend(q[:, c], k, v)])


def near(*args):
    return pl.pallas_call(
        near_kernel,
        out_shape=[out_of(NROWS, COLS, dtype=F32)] * 3,
        in_specs=[VMEM] * 10,
        out_specs=[VMEM] * 3,
        compiler_params=params(16),
        cost_estimate=cost(0),
        name="near",
    )(*args)


def across_kernel(q, nm, nl, na, far_zc, rest_z, m, l, acc):
    for h in range(HEADS):
        c, d = head_cols(h), value_cols(h)
        k, v = (
            jnp.concatenate([far_zc[FROWS:, cols], rest_z[:, cols]], 0) for cols in (c, d)
        )
        m[:, c], l[:, c], acc[:, c] = merge(
            [(nm[:, c], nl[:, c], na[:, c]), attend(q[:, c], k, v)]
        )


def across(*args):
    return pl.pallas_call(
        across_kernel,
        out_shape=[out_of(NROWS, COLS, dtype=F32)] * 3,
        in_specs=[VMEM] * 6,
        out_specs=[VMEM] * 3,
        compiler_params=params(16),
        cost_estimate=cost(0),
        name="across",
    )(*args)


def far_kernel(*refs):
    q, kv, out = refs[:4], refs[4:12], refs[12:]
    for part in out:
        part[:, COLS:] = jnp.zeros((FROWS, 3 * DH), BF16)
    for h in range(HEADS):
        c, d = head_cols(h), value_cols(h)
        qh = jnp.concatenate([x[:, c] for x in q], 0)
        k = jnp.concatenate([x[:, c] for x in kv], 0)
        v = jnp.concatenate([x[:, d] for x in kv], 0)
        m, l, o = attend(qh, k, v)
        o = (o * (1.0 / l)).astype(BF16)
        lse = (m + jnp.log2(l))[:, :1]
        first = lse.astype(BF16)
        left = lse - first.astype(F32)
        second = left.astype(BF16)
        third = (left - second.astype(F32)).astype(BF16)
        for i, part in enumerate(out):
            rows = slice(i * FROWS, (i + 1) * FROWS)
            part[:, c] = o[rows]
            for e, piece in enumerate((first, second, third)):
                col = COLS + e * DH + h
                part[:, col : col + 1] = piece[rows]


def far(*args):
    return pl.pallas_call(
        far_kernel,
        out_shape=[out_of(FROWS, SENT)] * 4,
        in_specs=[VMEM] * 12,
        out_specs=[VMEM] * 4,
        compiler_params=params(16),
        cost_estimate=cost(0),
        name="far",
    )(*args)


def fold_kernel(f0, f1, f2, f3, m, l, acc):
    fars = (f0, f1, f2, f3)
    lses = [
        sum(f[:, COLS + e * DH : COLS + (e + 1) * DH].astype(F32) for e in range(3)) for f in fars
    ]
    for h in range(HEADS):
        c = head_cols(h)
        m[:, c], l[:, c], acc[:, c] = merge(
            [
                (wide(x[:, h : h + 1]), jnp.ones((FROWS, DH), F32), f[:, c].astype(F32))
                for x, f in zip(lses, fars)
            ]
        )


def fold(*args):
    return pl.pallas_call(
        fold_kernel,
        out_shape=[out_of(FROWS, COLS, dtype=F32)] * 3,
        in_specs=[VMEM] * 4,
        out_specs=[VMEM] * 3,
        compiler_params=params(8),
        cost_estimate=cost(5),
        name="fold",
    )(*args)


def join_kernel(
    far_z, res, q, nm, nl, na, rest_zc, done0, done, fm, fl, fa, out, block, sems
):
    restored = []
    for h in range(HEADS):
        c, d = head_cols(h), value_cols(h)
        m, l, acc = merge(
            [(nm[:, c], nl[:, c], na[:, c]), attend(q[:, c], rest_zc[:, c], rest_zc[:, d])]
        )
        for b in range(BLOCKS):
            rows = slice(b * NEAR, (b + 1) * NEAR)
            mb, lb, ab = m[rows], l[rows], acc[rows]
            fr = slice(b * FAR, (b + 1) * FAR)
            _, lf, af = merge(
                [(mb[:FAR], lb[:FAR], ab[:FAR]), (fm[fr, c], fl[fr, c], fa[fr, c])]
            )
            restored.append(
                (
                    jnp.concatenate([af, ab[FAR:]], 0)
                    * (1.0 / jnp.concatenate([lf, lb[FAR:]], 0))
                ).astype(BF16)
            )
    copies = []
    for b in range(0, BLOCKS, 2):
        for h in range(HEADS):
            c = head_cols(h)
            pair = jnp.concatenate(restored[h * BLOCKS + b : h * BLOCKS + b + 2], 1)
            placed = dot(res[block_rows(h), OTHER:], pair).astype(BF16)
            for i in range(2):
                rest = done0[:, c] if b + i == 0 else done[block_rows(b + i - 1), c]
                block[block_rows(b + i), c] = rest + placed[:, i * DH : (i + 1) * DH]
        for i in range(2):
            rows = block_rows(b + i)
            copies.append(
                pltpu.make_async_copy(block.at[rows, :], out.at[rows, :], sems.at[b + i])
            )
            copies[-1].start()
    for copy in copies:
        copy.wait()


def join(*args):
    return pl.pallas_call(
        join_kernel,
        out_shape=out_of(TOK, COLS),
        in_specs=[VMEM] * 12,
        out_specs=HBM,
        scratch_shapes=[pltpu.VMEM((TOK, COLS), BF16), pltpu.SemaphoreType.DMA((BLOCKS,))],
        compiler_params=params(16),
        cost_estimate=cost(0),
        name="join",
    )(*args)


def place(x, y, z, core):
    return ((x % 4 * 4 + y % 4) * 2 + z % 2) * 2 + core


def moves(dx=0, dy=0, dz=0, dcore=0):
    return [
        (place(x, y, z, core), place(x + dx, y + dy, z + dz, (core + dcore) % 2))
        for x in range(4)
        for y in range(4)
        for z in range(2)
        for core in range(2)
    ]


def send(value, **shift):
    return lax.ppermute(value, "seq", moves(**shift))


def shards(q, k, v, off):
    offs, kv_far, kv_rest, kv_near, halo = extract(off, k, v)
    far_z = send(kv_far, dz=1)
    near_c = send(kv_near, dcore=1)
    halo_c = send(halo, dcore=1)
    qp, qn, qf, res = permute_queries(offs, q)
    halo, near_c = lax.optimization_barrier((halo, near_c))
    halo = lax.ppermute(halo, "seq", [(s, s + 1) for s in range(1, 63, 2)])
    qf, halo_c = lax.optimization_barrier((qf, halo_c))
    qs = [send(qf, dy=s) for s in (2, 1, -1)]
    far_z, *qs = lax.optimization_barrier((far_z, *qs))
    own = join_far(kv_far, far_z)
    kv_rest, _ = lax.optimization_barrier((kv_rest, own))
    gathered = [send(own, dx=s) for s in (2, 1, -1)]
    rest_z = send(kv_rest, dz=1)
    done, *kept = local(res, qp, k, v)
    done0, *halo_state = halo_fold(res, qp, *kept, halo_c, halo)
    own, _ = lax.optimization_barrier((own, done0))
    own_c = send(own, dcore=1)
    gathered, _ = lax.optimization_barrier((gathered, done0))
    crossed = [send(x, dcore=1) for x in gathered]
    parts = far(qf, *qs, own, *gathered, own_c, *crossed)
    back = [parts[0]] + [send(p, dy=-s) for p, s in zip(parts[1:], (2, 1, -1))]
    folded = fold(*back)
    qn, _ = lax.optimization_barrier((qn, parts[0]))
    state = near(qn, *kept, *halo_state, kv_near, near_c, far_z)
    rest_z, _ = lax.optimization_barrier((rest_z, state[0]))
    rest_zc = send(rest_z, dcore=1)
    state = across(qn, *state, own_c, rest_z)
    return join(far_z, res, qn, *state, rest_zc, done0, done, *folded)


def solution(mesh):
    placed = (P("seq", "head"), P("seq", "head"), P("seq", "head"), P("head"))
    return jax.shard_map(
        shards, mesh=mesh, in_specs=placed, out_specs=P("seq", "head"), check_vma=False
    )
```

```python
import functools

import jax
import jax.numpy as jnp
from jax import lax
from jax.experimental import pallas as pl
from jax.experimental.pallas import tpu as pltpu
from jax.sharding import PartitionSpec as P

HEADS = 4
DH = 128
W0 = 256
BLOCKS = 4
R1 = 4
R2 = 16
TOK = 1024
COLS = 512
NEAR = 64
FAR = 16
REST = NEAR - FAR
OTHER = W0 - NEAR
NROWS = NEAR * BLOCKS
FROWS = FAR * BLOCKS
KEPT = OTHER + NROWS
HALF = COLS // 2
SENT = HALF + DH
SCALE2 = 128**-0.5 * 1.4426950408889634
F32 = jnp.float32
BF16 = jnp.bfloat16

VMEM = pl.BlockSpec(memory_space=pltpu.VMEM)
HBM = pl.BlockSpec(memory_space=pltpu.HBM)


def out_of(*shape, dtype=BF16):
    return jax.ShapeDtypeStruct(shape, dtype)


def params(mib):
    return pltpu.CompilerParams(vmem_limit_bytes=mib << 20)


def cost(us):
    return pl.CostEstimate(flops=int(us * 1e9), bytes_accessed=1000, transcendentals=0)


def source_row(index, offset):
    order = index >> 4
    residue = ((order & 3) << 2) + (((order >> 2) + 1) & 3)
    return ((index & 15) << 4) + ((offset + residue) & 15)


def select_matrix(offset, start, count):
    index = lax.broadcasted_iota(jnp.int32, (count, W0), 0) + start
    row = lax.broadcasted_iota(jnp.int32, (count, W0), 1)
    return jnp.where(row == source_row(index, offset), 1.0, 0.0).astype(BF16)


def restore_matrix(offset, start, count):
    index = lax.broadcasted_iota(jnp.int32, (W0, count), 1) + start
    row = lax.broadcasted_iota(jnp.int32, (W0, count), 0)
    return jnp.where(row == source_row(index, offset), 1.0, 0.0).astype(BF16)


def dot(a, b):
    return jnp.dot(a, b, preferred_element_type=F32)


def dot_nt(a, b):
    return lax.dot_general(a, b, (((1,), (1,)), ((), ())), preferred_element_type=F32)


def wide(column):
    return jnp.broadcast_to(column, (column.shape[0], DH))


def attend(q, k, v):
    s = dot_nt(q, k) * SCALE2
    m = jnp.max(s, axis=1, keepdims=True)
    p = jnp.exp2(s - m)
    l = jnp.sum(p, axis=1, keepdims=True)
    return wide(m), wide(l), dot(p.astype(BF16), v)


def merge(states):
    m = functools.reduce(jnp.maximum, [s[0] for s in states])
    scales = [jnp.exp2(s[0] - m) for s in states]
    l = sum(s[1] * c for s, c in zip(states, scales))
    acc = sum(s[2] * c for s, c in zip(states, scales))
    return m, l, acc


def head_cols(h):
    return slice(h * DH, (h + 1) * DH)


def value_cols(h):
    return slice(COLS + h * DH, COLS + (h + 1) * DH)


def block_rows(b):
    return slice(b * W0, (b + 1) * W0)


def offset_rows(offs, h, width):
    row = offs[h : h + 1, :]
    return jnp.concatenate([row] * (width // DH), 1) if width > DH else row[:, :width]


def extract_kernel(
    off_hbm, k_hbm, v_hbm, offs, kv_far, kv_rest, kv_near, halo, off, k, v, k32, v32, off_sem, sems
):
    off_copy = pltpu.make_async_copy(off_hbm, off, off_sem)
    off_copy.start()
    copies = {}
    for b in reversed(range(BLOCKS)):
        for i, (src, dst) in enumerate(((k_hbm, k), (v_hbm, v))):
            copies[i, b] = pltpu.make_async_copy(
                src.at[block_rows(b), :], dst.at[block_rows(b), :], sems.at[i, b]
            )
            copies[i, b].start()
    off_copy.wait()
    for h in range(HEADS):
        offs[h : h + 1, :] = jnp.full((1, DH), off[h], jnp.int32)
    for b in reversed(range(BLOCKS)):
        rows = block_rows(b)
        for i, (src, dst) in enumerate(((k, k32), (v, v32))):
            copies[i, b].wait()
            if b == BLOCKS - 1:
                copies[i, BLOCKS] = pltpu.make_async_copy(
                    src.at[rows, :], halo.at[:, i * COLS : (i + 1) * COLS], sems.at[i, BLOCKS]
                )
                copies[i, BLOCKS].start()
            for h in range(HEADS):
                dst[h, rows, :] = src[rows, head_cols(h)].astype(F32)
    for h in range(HEADS):
        for a in range(R2 // R1):
            start = (off[h] + R1 * a) & (R2 - 1)
            for src, cols in ((k32, head_cols(h)), (v32, value_cols(h))):
                part = src[h, pl.ds(start, FROWS, stride=R2), :].astype(BF16)
                kv_near[a * FROWS : (a + 1) * FROWS, cols] = part
                if a == 0:
                    kv_far[:, cols] = part
                else:
                    kv_rest[(a - 1) * FROWS : a * FROWS, cols] = part
    for i in range(2):
        copies[i, BLOCKS].wait()


def extract(*args):
    return pl.pallas_call(
        extract_kernel,
        out_shape=[
            out_of(8, DH, dtype=jnp.int32),
            out_of(FROWS, 2 * COLS),
            out_of(REST * BLOCKS, 2 * COLS),
            out_of(NROWS, 2 * COLS),
            out_of(W0, 2 * COLS),
        ],
        in_specs=[HBM] * 3,
        out_specs=[VMEM] * 4 + [HBM],
        scratch_shapes=[
            pltpu.SMEM((HEADS,), jnp.int32),
            pltpu.VMEM((TOK, COLS), BF16),
            pltpu.VMEM((TOK, COLS), BF16),
            pltpu.VMEM((HEADS, TOK, DH), F32),
            pltpu.VMEM((HEADS, TOK, DH), F32),
            pltpu.SemaphoreType.DMA,
            pltpu.SemaphoreType.DMA((2, BLOCKS + 1)),
        ],
        compiler_params=params(59),
        cost_estimate=cost(0),
        name="extract",
    )(*args)


def queries_kernel(offs, q_hbm, qp, qn, q_keep, q_give, res, q, sems):
    core = lax.axis_index("seq") & 1
    qf = {}
    copies = []
    for b in range(BLOCKS):
        copies.append(
            pltpu.make_async_copy(q_hbm.at[block_rows(b), :], q.at[block_rows(b), :], sems.at[b])
        )
        copies[-1].start()
    sels = []
    for h in range(HEADS):
        offset = offset_rows(offs, h, W0)
        sels.append(select_matrix(offset, 0, W0))
        res[block_rows(h), :] = restore_matrix(offset, 0, W0)
    for b in range(0, BLOCKS, 2):
        copies[b].wait()
        copies[b + 1].wait()
        for h in range(HEADS):
            c = head_cols(h)
            pair = jnp.concatenate([q[block_rows(b), c], q[block_rows(b + 1), c]], 1)
            moved = dot(sels[h], pair).astype(BF16)
            for i in range(2):
                part = moved[:, i * DH : (i + 1) * DH]
                qp[block_rows(b + i), c] = part
                qn[(b + i) * NEAR : (b + i + 1) * NEAR, c] = part[OTHER:]
                qf[b + i, h] = part[OTHER : OTHER + FAR]
    for b in range(BLOCKS):
        rows = slice(b * FAR, (b + 1) * FAR)
        for g in range(HEADS // 2):
            low, high = qf[b, g], qf[b, g + HEADS // 2]
            q_keep[rows, head_cols(g)] = jnp.where(core == 0, low, high)
            q_give[rows, head_cols(g)] = jnp.where(core == 0, high, low)


def permute_queries(*args):
    return pl.pallas_call(
        queries_kernel,
        out_shape=[
            out_of(TOK, COLS),
            out_of(NROWS, COLS),
            out_of(FROWS, HALF),
            out_of(FROWS, HALF),
            out_of(HEADS * W0, W0),
        ],
        in_specs=[VMEM, HBM],
        out_specs=[VMEM] * 5,
        scratch_shapes=[pltpu.VMEM((TOK, COLS), BF16), pltpu.SemaphoreType.DMA((BLOCKS,))],
        compiler_params=params(16),
        cost_estimate=cost(12),
        name="queries",
    )(*args)


def pick(ref, core, start):
    return jnp.where(core == 0, ref[:, start : start + HALF], ref[:, start + HALF : start + COLS])


def split_kernel(far_z, keep, give):
    core = lax.axis_index("seq") & 1
    for start in (0, COLS):
        cols = slice(start // 2, start // 2 + HALF)
        keep[:, cols] = pick(far_z, core, start)
        give[:, cols] = pick(far_z, 1 - core, start)


def split_far(*args):
    return pl.pallas_call(
        split_kernel,
        out_shape=[out_of(FROWS, COLS)] * 2,
        in_specs=[VMEM],
        out_specs=[VMEM] * 2,
        compiler_params=params(8),
        cost_estimate=cost(0),
        name="split",
    )(*args)


def keys_kernel(kv_far, near_c, keep, given, own):
    core = lax.axis_index("seq") & 1
    for i, src in enumerate((kv_far, near_c.at[:FROWS, :])):
        rows = slice(i * FROWS, (i + 1) * FROWS)
        own[rows, :HALF] = pick(src, core, 0)
        own[rows, HALF:] = pick(src, core, COLS)
    own[2 * FROWS : 3 * FROWS, :] = keep[...]
    own[3 * FROWS :, :] = given[...]


def pick_keys(*args):
    return pl.pallas_call(
        keys_kernel,
        out_shape=out_of(4 * FROWS, COLS),
        in_specs=[VMEM] * 4,
        out_specs=VMEM,
        compiler_params=params(8),
        cost_estimate=cost(0),
        name="keys",
    )(*args)


def half_kernel(keep, given, out):
    core = lax.axis_index("seq") & 1
    out[:FROWS, :] = jnp.where(core == 0, keep[...], given[...])
    out[FROWS:, :] = jnp.where(core == 0, given[...], keep[...])


def pick_queries(*args):
    return pl.pallas_call(
        half_kernel,
        out_shape=out_of(2 * FROWS, HALF),
        in_specs=[VMEM] * 2,
        out_specs=VMEM,
        compiler_params=params(8),
        cost_estimate=cost(0),
        name="half",
    )(*args)


def local_kernel(res, q, k, v, done, km, kl, ka):
    for h in range(HEADS):
        c = head_cols(h)
        qs = [q[block_rows(b), c] for b in range(BLOCKS)]
        scores = [[] for _ in range(BLOCKS)]
        for j in range(BLOCKS):
            users = qs[j : j + 2]
            s = dot_nt(jnp.concatenate(users, 0), k[block_rows(j), c]) * SCALE2
            for i in range(len(users)):
                scores[j + i].append(s[i * W0 : (i + 1) * W0])
        ms, ls, ps = [], [], []
        for b in range(BLOCKS):
            m = functools.reduce(
                jnp.maximum, [jnp.max(s, axis=1, keepdims=True) for s in scores[b]]
            )
            p = [jnp.exp2(s - m) for s in scores[b]]
            ms.append(m)
            ls.append(sum(jnp.sum(x, axis=1, keepdims=True) for x in p))
            ps.append([x.astype(BF16) for x in p])
        accs = [None] * BLOCKS
        for j in range(BLOCKS):
            users = [ps[j][-1]] + ([ps[j + 1][0]] if j + 1 < BLOCKS else [])
            o = dot(jnp.concatenate(users, 0), v[block_rows(j), c])
            for i in range(len(users)):
                part = o[i * W0 : (i + 1) * W0]
                accs[j + i] = part if accs[j + i] is None else accs[j + i] + part
        km[:W0, c], kl[:W0, c], ka[:W0, c] = wide(ms[0]), wide(ls[0]), accs[0]
        rest = []
        for b in range(1, BLOCKS):
            near = slice(OTHER + b * NEAR, OTHER + (b + 1) * NEAR)
            km[near, c] = wide(ms[b][OTHER:])
            kl[near, c] = wide(ls[b][OTHER:])
            ka[near, c] = accs[b][OTHER:]
            rest.append((accs[b][:OTHER] * (1.0 / ls[b][:OTHER])).astype(BF16))
        restore = res[block_rows(h), :OTHER]
        pair = dot(restore, jnp.concatenate(rest[:2], 1)).astype(BF16)
        done[0:W0, c] = pair[:, :DH]
        done[W0 : 2 * W0, c] = pair[:, DH:]
        done[2 * W0 :, c] = dot(restore, rest[2]).astype(BF16)


def local(*args):
    state = out_of(KEPT, COLS, dtype=F32)
    return pl.pallas_call(
        local_kernel,
        out_shape=[
            out_of(TOK - W0, COLS),
            state,
            state,
            state,
        ],
        in_specs=[VMEM] * 4,
        out_specs=[VMEM] * 4,
        compiler_params=params(16),
        cost_estimate=cost(1),
        name="local",
    )(*args)


def halo_kernel(res, q, km, kl, ka, halo_c, halo, done, hm, hl, ha):
    position = lax.axis_index("seq")
    from_core = (position & 1) == 1
    has_halo = position > 0
    for h in range(HEADS):
        c, d = head_cols(h), value_cols(h)
        hk = jnp.where(from_core, halo_c[:, c], halo[:, c])
        hv = jnp.where(from_core, halo_c[:, d], halo[:, d])
        m = km[:W0, c]
        s = jnp.where(has_halo, dot_nt(q[:W0, c], hk) * SCALE2, -jnp.inf)
        m_new = jnp.maximum(m, wide(jnp.max(s, axis=1, keepdims=True)))
        p = jnp.exp2(s - jnp.concatenate([m_new, m_new], 1))
        scale = jnp.exp2(m - m_new)
        l = kl[:W0, c] * scale + wide(jnp.sum(p, axis=1, keepdims=True))
        acc = ka[:W0, c] * scale + dot(p.astype(BF16), hv)
        hm[:, c], hl[:, c], ha[:, c] = m_new[OTHER:], l[OTHER:], acc[OTHER:]
        rest = (acc[:OTHER] * (1.0 / l[:OTHER])).astype(BF16)
        done[:, c] = dot(res[block_rows(h), :OTHER], rest).astype(BF16)


def halo_fold(*args):
    state = out_of(NEAR, COLS, dtype=F32)
    return pl.pallas_call(
        halo_kernel,
        out_shape=[out_of(W0, COLS), state, state, state],
        in_specs=[VMEM] * 7,
        out_specs=[VMEM] * 4,
        compiler_params=params(16),
        cost_estimate=cost(0),
        name="halo",
    )(*args)


def near_kernel(q, km, kl, ka, near, near_c, far_z, m, l, acc):
    for h in range(HEADS):
        c, d = head_cols(h), value_cols(h)
        k, v = (
            jnp.concatenate([near[:, cols], near_c[:, cols], far_z[:, cols]], 0)
            for cols in (c, d)
        )
        state = attend(q[:, c], k, v)
        later = merge([(km[W0:, c], kl[W0:, c], ka[W0:, c]), tuple(x[NEAR:] for x in state)])
        for ref, first, rest in zip((m, l, acc), state, later):
            ref[:NEAR, c] = first[:NEAR]
            ref[NEAR:, c] = rest


def near(*args):
    return pl.pallas_call(
        near_kernel,
        out_shape=[out_of(NROWS, COLS, dtype=F32)] * 3,
        in_specs=[VMEM] * 7,
        out_specs=[VMEM] * 3,
        compiler_params=params(16),
        cost_estimate=cost(0),
        name="near",
    )(*args)


def across_kernel(q, nm, nl, na, given, other, rest_z, rest_zc, m, l, acc):
    core = lax.axis_index("seq") & 1
    for h in range(HEADS):
        c, d = head_cols(h), value_cols(h)
        k, v = (
            jnp.concatenate(
                [
                    jnp.where(core == h // 2, given[:, half], other[:, half]),
                    rest_z[:, cols],
                    rest_zc[:, cols],
                ],
                0,
            )
            for cols, half in (
                (c, head_cols(h % 2)),
                (d, slice(HALF + h % 2 * DH, HALF + (h % 2 + 1) * DH)),
            )
        )
        m[:, c], l[:, c], acc[:, c] = merge(
            [(nm[:, c], nl[:, c], na[:, c]), attend(q[:, c], k, v)]
        )


def across(*args):
    return pl.pallas_call(
        across_kernel,
        out_shape=[out_of(NROWS, COLS, dtype=F32)] * 3,
        in_specs=[VMEM] * 8,
        out_specs=[VMEM] * 3,
        compiler_params=params(16),
        cost_estimate=cost(0),
        name="across",
    )(*args)


def far_kernel(*refs):
    q, kv, out = refs[:4], refs[4:8], refs[8:]
    n = 2 * FROWS
    for part in out:
        part[:, HALF:] = jnp.zeros((n, DH), BF16)
    for g in range(HEADS // 2):
        c = head_cols(g)
        d = slice(HALF + g * DH, HALF + (g + 1) * DH)
        qh = jnp.concatenate([x[:, c] for x in q], 0)
        k = jnp.concatenate([x[:, c] for x in kv], 0)
        v = jnp.concatenate([x[:, d] for x in kv], 0)
        m, l, o = attend(qh, k, v)
        o = (o * (1.0 / l)).astype(BF16)
        lse = (m + jnp.log2(l))[:, :1]
        first = lse.astype(BF16)
        left = lse - first.astype(F32)
        second = left.astype(BF16)
        third = (left - second.astype(F32)).astype(BF16)
        for i, part in enumerate(out):
            rows = slice(i * n, (i + 1) * n)
            part[:, c] = o[rows]
            for e, piece in enumerate((first, second, third)):
                col = HALF + 2 * e + g
                part[:, col : col + 1] = piece[rows]


def far(*args):
    return pl.pallas_call(
        far_kernel,
        out_shape=[out_of(2 * FROWS, SENT)] * 4,
        in_specs=[VMEM] * 8,
        out_specs=[VMEM] * 4,
        compiler_params=params(24),
        cost_estimate=cost(0),
        name="far",
    )(*args)


def fold_kernel(f0, f1, f2, f3, out):
    for g in range(HEADS // 2):
        c = head_cols(g)
        states = []
        for f in (f0, f1, f2, f3):
            lse = sum(
                f[:, HALF + 2 * e + g : HALF + 2 * e + g + 1].astype(F32) for e in range(3)
            )
            states.append((wide(lse), jnp.ones((2 * FROWS, DH), F32), f[:, c].astype(F32)))
        m, l, acc = merge(states)
        out[:, c] = acc * (1.0 / l)
        out[:, HALF + g * DH : HALF + (g + 1) * DH] = m + jnp.log2(l)


def fold(*args):
    return pl.pallas_call(
        fold_kernel,
        out_shape=out_of(2 * FROWS, COLS, dtype=F32),
        in_specs=[VMEM] * 4,
        out_specs=VMEM,
        compiler_params=params(8),
        cost_estimate=cost(0),
        name="fold",
    )(*args)


def join_kernel(
    far_z, res, hm, hl, ha, nm, nl, na, done0, done, mine, mine_c, out, block, sems
):
    core = lax.axis_index("seq") & 1
    restored = []
    for h in range(HEADS):
        c = head_cols(h)
        m, l, acc = nm[:, c], nl[:, c], na[:, c]
        g = h % 2
        fo, fm = (
            jnp.where(
                core == h // 2,
                jnp.where(core == 0, mine[:FROWS, cols], mine[FROWS:, cols]),
                jnp.where(core == 0, mine_c[:FROWS, cols], mine_c[FROWS:, cols]),
            )
            for cols in (head_cols(g), slice(HALF + g * DH, HALF + (g + 1) * DH))
        )
        for b in range(BLOCKS):
            rows = slice(b * NEAR, (b + 1) * NEAR)
            mb, lb, ab = m[rows], l[rows], acc[rows]
            if b == 0:
                mb, lb, ab = merge([(hm[:, c], hl[:, c], ha[:, c]), (mb, lb, ab)])
            fr = slice(b * FAR, (b + 1) * FAR)
            _, lf, af = merge([(mb[:FAR], lb[:FAR], ab[:FAR]), (fm[fr], 1.0, fo[fr])])
            restored.append(
                (
                    jnp.concatenate([af, ab[FAR:]], 0)
                    * (1.0 / jnp.concatenate([lf, lb[FAR:]], 0))
                ).astype(BF16)
            )
    copies = []
    for b in range(0, BLOCKS, 2):
        for h in range(HEADS):
            c = head_cols(h)
            pair = jnp.concatenate(restored[h * BLOCKS + b : h * BLOCKS + b + 2], 1)
            placed = dot(res[block_rows(h), OTHER:], pair).astype(BF16)
            for i in range(2):
                rest = done0[:, c] if b + i == 0 else done[block_rows(b + i - 1), c]
                block[block_rows(b + i), c] = rest + placed[:, i * DH : (i + 1) * DH]
        for i in range(2):
            rows = block_rows(b + i)
            copies.append(
                pltpu.make_async_copy(block.at[rows, :], out.at[rows, :], sems.at[b + i])
            )
            copies[-1].start()
    for copy in copies:
        copy.wait()


def join(*args):
    return pl.pallas_call(
        join_kernel,
        out_shape=out_of(TOK, COLS),
        in_specs=[VMEM] * 12,
        out_specs=HBM,
        scratch_shapes=[pltpu.VMEM((TOK, COLS), BF16), pltpu.SemaphoreType.DMA((BLOCKS,))],
        compiler_params=params(16),
        cost_estimate=cost(0),
        name="join",
    )(*args)


def place(x, y, z, core):
    return ((x % 4 * 4 + y % 4) * 2 + z % 2) * 2 + core


def moves(dx=0, dy=0, dz=0, dcore=0):
    return [
        (place(x, y, z, core), place(x + dx, y + dy, z + dz, (core + dcore) % 2))
        for x in range(4)
        for y in range(4)
        for z in range(2)
        for core in range(2)
    ]


def send(value, **shift):
    return lax.ppermute(value, "seq", moves(**shift))


def turn(value, step, keys):
    pairs = []
    for x in range(4):
        for y in range(4):
            for z in range(2):
                for core in range(2):
                    dx, dy = (step, 0) if (core == 0) == keys else (0, step)
                    pairs.append((place(x, y, z, core), place(x + dx, y + dy, z, core)))
    return lax.ppermute(value, "seq", pairs)


def shards(q, k, v, off):
    offs, kv_far, kv_rest, kv_near, halo = extract(off, k, v)
    far_z = send(kv_far, dz=1)
    near_c = send(kv_near, dcore=1)
    halo_c = send(halo, dcore=1)
    kv_rest, near_c = lax.optimization_barrier((kv_rest, near_c))
    rest_z = send(kv_rest, dz=1)
    qp, qn, q_keep, q_give, res = permute_queries(offs, q)
    q_give, halo_c = lax.optimization_barrier((q_give, halo_c))
    qm = pick_queries(q_keep, send(q_give, dcore=1))
    steps = (2, 1, -1)
    qs = [turn(qm, s, False) for s in steps]
    done, *kept = local(res, qp, k, v)
    far_z, *_ = lax.optimization_barrier((far_z, done, *qs))
    keep, give = split_far(far_z)
    given = send(give, dcore=1)
    own = pick_keys(kv_far, near_c, keep, given)
    gathered = [own] + [turn(own, s, True) for s in steps]
    halo, _ = lax.optimization_barrier((halo, own))
    halo = lax.ppermute(halo, "seq", [(s, s + 1) for s in range(1, 63, 2)])
    rest_z, *_ = lax.optimization_barrier((rest_z, *gathered, done))
    parts = far(qm, *qs, *gathered)
    rest_zc = send(rest_z, dcore=1)
    rest_zc, *parts = lax.optimization_barrier((rest_zc, *parts))
    keep, *_ = lax.optimization_barrier((keep, *parts))
    other = send(keep, dcore=1)
    back = [parts[0]] + [turn(p, -s, False) for p, s in zip(parts[1:], steps)]
    mine = fold(*back)
    state = near(qn, *kept, kv_near, near_c, far_z)
    state = across(qn, *state, given, other, rest_z, rest_zc)
    done0, *halo_state = halo_fold(res, qp, *kept, halo_c, halo)
    mine, *_ = lax.optimization_barrier((mine, halo, state[0]))
    mine_c = send(mine, dcore=1)
    return join(far_z, res, *halo_state, *state, done0, done, mine, mine_c)


def solution(mesh):
    placed = (P("seq", "head"), P("seq", "head"), P("seq", "head"), P("head"))
    return jax.shard_map(
        shards, mesh=mesh, in_specs=placed, out_specs=P("seq", "head"), check_vma=False
    )
```

```python
import functools

import jax
import jax.numpy as jnp
from jax import lax
from jax.experimental import pallas as pl
from jax.experimental.pallas import tpu as pltpu
from jax.sharding import PartitionSpec as P

HEADS = 4
DH = 128
W0 = 256
BLOCKS = 4
R1 = 4
R2 = 16
TOK = 1024
COLS = 512
NEAR = 64
FAR = 16
REST = NEAR - FAR
OTHER = W0 - NEAR
NROWS = NEAR * BLOCKS
FROWS = FAR * BLOCKS
KEPT = OTHER + NROWS
HALF = COLS // 2
SENT = HALF + DH
SCALE2 = 128**-0.5 * 1.4426950408889634
F32 = jnp.float32
BF16 = jnp.bfloat16

VMEM = pl.BlockSpec(memory_space=pltpu.VMEM)
HBM = pl.BlockSpec(memory_space=pltpu.HBM)


def out_of(*shape, dtype=BF16):
    return jax.ShapeDtypeStruct(shape, dtype)


def params(mib):
    return pltpu.CompilerParams(vmem_limit_bytes=mib << 20)


def cost(us):
    return pl.CostEstimate(flops=int(us * 1e9), bytes_accessed=1000, transcendentals=0)


def source_row(index, offset):
    order = index >> 4
    residue = ((order & 3) << 2) + (((order >> 2) + 1) & 3)
    return ((index & 15) << 4) + ((offset + residue) & 15)


def select_matrix(offset, start, count):
    index = lax.broadcasted_iota(jnp.int32, (count, W0), 0) + start
    row = lax.broadcasted_iota(jnp.int32, (count, W0), 1)
    return jnp.where(row == source_row(index, offset), 1.0, 0.0).astype(BF16)


def restore_matrix(offset, start, count):
    index = lax.broadcasted_iota(jnp.int32, (W0, count), 1) + start
    row = lax.broadcasted_iota(jnp.int32, (W0, count), 0)
    return jnp.where(row == source_row(index, offset), 1.0, 0.0).astype(BF16)


def dot(a, b):
    return jnp.dot(a, b, preferred_element_type=F32)


def dot_nt(a, b):
    return lax.dot_general(a, b, (((1,), (1,)), ((), ())), preferred_element_type=F32)


def wide(column):
    return jnp.broadcast_to(column, (column.shape[0], DH))


def staged(first, second):
    ready = first(0)
    for h in range(HEADS):
        later = first(h + 1) if h + 1 < HEADS else None
        second(h, ready)
        ready = later


def weigh(s, v):
    m = jnp.max(s, axis=1, keepdims=True)
    p = jnp.exp2(s - m)
    l = jnp.sum(p, axis=1, keepdims=True)
    return wide(m), wide(l), dot(p.astype(BF16), v)


def merge(states):
    m = functools.reduce(jnp.maximum, [s[0] for s in states])
    scales = [jnp.exp2(s[0] - m) for s in states]
    l = sum(s[1] * c for s, c in zip(states, scales))
    acc = sum(s[2] * c for s, c in zip(states, scales))
    return m, l, acc


def head_cols(h):
    return slice(h * DH, (h + 1) * DH)


def value_cols(h):
    return slice(COLS + h * DH, COLS + (h + 1) * DH)


def block_rows(b):
    return slice(b * W0, (b + 1) * W0)


def offset_rows(offs, h, width):
    row = offs[h : h + 1, :]
    return jnp.concatenate([row] * (width // DH), 1) if width > DH else row[:, :width]


def extract_kernel(
    off_hbm, k_hbm, v_hbm, offs, kv_far, kv_rest, kv_near, halo, off, k, v, k32, v32, off_sem, sems
):
    off_copy = pltpu.make_async_copy(off_hbm, off, off_sem)
    off_copy.start()
    copies = {}
    for b in reversed(range(BLOCKS)):
        for i, (src, dst) in enumerate(((k_hbm, k), (v_hbm, v))):
            copies[i, b] = pltpu.make_async_copy(
                src.at[block_rows(b), :], dst.at[block_rows(b), :], sems.at[i, b]
            )
            copies[i, b].start()
    off_copy.wait()
    for h in range(HEADS):
        offs[h : h + 1, :] = jnp.full((1, DH), off[h], jnp.int32)
    for b in reversed(range(BLOCKS)):
        rows = block_rows(b)
        for i, (src, dst) in enumerate(((k, k32), (v, v32))):
            copies[i, b].wait()
            if b == BLOCKS - 1:
                copies[i, BLOCKS] = pltpu.make_async_copy(
                    src.at[rows, :], halo.at[:, i * COLS : (i + 1) * COLS], sems.at[i, BLOCKS]
                )
                copies[i, BLOCKS].start()
            for h in range(HEADS):
                dst[h, rows, :] = src[rows, head_cols(h)].astype(F32)
    for h in range(HEADS):
        for a in range(R2 // R1):
            start = (off[h] + R1 * a) & (R2 - 1)
            for src, cols in ((k32, head_cols(h)), (v32, value_cols(h))):
                part = src[h, pl.ds(start, FROWS, stride=R2), :].astype(BF16)
                kv_near[a * FROWS : (a + 1) * FROWS, cols] = part
                if a == 0:
                    kv_far[:, cols] = part
                else:
                    kv_rest[(a - 1) * FROWS : a * FROWS, cols] = part
    for i in range(2):
        copies[i, BLOCKS].wait()


def extract(*args):
    return pl.pallas_call(
        extract_kernel,
        out_shape=[
            out_of(8, DH, dtype=jnp.int32),
            out_of(FROWS, 2 * COLS),
            out_of(REST * BLOCKS, 2 * COLS),
            out_of(NROWS, 2 * COLS),
            out_of(W0, 2 * COLS),
        ],
        in_specs=[HBM] * 3,
        out_specs=[VMEM] * 4 + [HBM],
        scratch_shapes=[
            pltpu.SMEM((HEADS,), jnp.int32),
            pltpu.VMEM((TOK, COLS), BF16),
            pltpu.VMEM((TOK, COLS), BF16),
            pltpu.VMEM((HEADS, TOK, DH), F32),
            pltpu.VMEM((HEADS, TOK, DH), F32),
            pltpu.SemaphoreType.DMA,
            pltpu.SemaphoreType.DMA((2, BLOCKS + 1)),
        ],
        compiler_params=params(59),
        cost_estimate=cost(0),
        name="extract",
    )(*args)


def queries_kernel(offs, q_hbm, qp, qn, q_keep, q_give, res, q, sems):
    core = lax.axis_index("seq") & 1
    qf = {}
    copies = []
    for b in range(BLOCKS):
        copies.append(
            pltpu.make_async_copy(q_hbm.at[block_rows(b), :], q.at[block_rows(b), :], sems.at[b])
        )
        copies[-1].start()
    sels = []
    for h in range(HEADS):
        offset = offset_rows(offs, h, W0)
        sels.append(select_matrix(offset, 0, W0))
        res[block_rows(h), :] = restore_matrix(offset, 0, W0)
    for b in range(0, BLOCKS, 2):
        copies[b].wait()
        copies[b + 1].wait()
        for h in range(HEADS):
            c = head_cols(h)
            pair = jnp.concatenate([q[block_rows(b), c], q[block_rows(b + 1), c]], 1)
            moved = dot(sels[h], pair).astype(BF16)
            for i in range(2):
                part = moved[:, i * DH : (i + 1) * DH]
                qp[block_rows(b + i), c] = part
                qn[(b + i) * NEAR : (b + i + 1) * NEAR, c] = part[OTHER:]
                qf[b + i, h] = part[OTHER : OTHER + FAR]
    for b in range(BLOCKS):
        rows = slice(b * FAR, (b + 1) * FAR)
        for g in range(HEADS // 2):
            low, high = qf[b, g], qf[b, g + HEADS // 2]
            q_keep[rows, head_cols(g)] = jnp.where(core == 0, low, high)
            q_give[rows, head_cols(g)] = jnp.where(core == 0, high, low)


def permute_queries(*args):
    return pl.pallas_call(
        queries_kernel,
        out_shape=[
            out_of(TOK, COLS),
            out_of(NROWS, COLS),
            out_of(FROWS, HALF),
            out_of(FROWS, HALF),
            out_of(HEADS * W0, W0),
        ],
        in_specs=[VMEM, HBM],
        out_specs=[VMEM] * 5,
        scratch_shapes=[pltpu.VMEM((TOK, COLS), BF16), pltpu.SemaphoreType.DMA((BLOCKS,))],
        compiler_params=params(16),
        cost_estimate=cost(12),
        name="queries",
    )(*args)


def pick(ref, core, start):
    return jnp.where(core == 0, ref[:, start : start + HALF], ref[:, start + HALF : start + COLS])


def split_kernel(far_z, keep, give):
    core = lax.axis_index("seq") & 1
    for start in (0, COLS):
        cols = slice(start // 2, start // 2 + HALF)
        keep[:, cols] = pick(far_z, core, start)
        give[:, cols] = pick(far_z, 1 - core, start)


def split_far(*args):
    return pl.pallas_call(
        split_kernel,
        out_shape=[out_of(FROWS, COLS)] * 2,
        in_specs=[VMEM],
        out_specs=[VMEM] * 2,
        compiler_params=params(8),
        cost_estimate=cost(0),
        name="split",
    )(*args)


def keys_kernel(kv_far, near_c, keep, given, own):
    core = lax.axis_index("seq") & 1
    for i, src in enumerate((kv_far, near_c.at[:FROWS, :])):
        rows = slice(i * FROWS, (i + 1) * FROWS)
        own[rows, :HALF] = pick(src, core, 0)
        own[rows, HALF:] = pick(src, core, COLS)
    own[2 * FROWS : 3 * FROWS, :] = keep[...]
    own[3 * FROWS :, :] = given[...]


def pick_keys(*args):
    return pl.pallas_call(
        keys_kernel,
        out_shape=out_of(4 * FROWS, COLS),
        in_specs=[VMEM] * 4,
        out_specs=VMEM,
        compiler_params=params(8),
        cost_estimate=cost(0),
        name="keys",
    )(*args)


def half_kernel(keep, given, out):
    core = lax.axis_index("seq") & 1
    out[:FROWS, :] = jnp.where(core == 0, keep[...], given[...])
    out[FROWS:, :] = jnp.where(core == 0, given[...], keep[...])


def pick_queries(*args):
    return pl.pallas_call(
        half_kernel,
        out_shape=out_of(2 * FROWS, HALF),
        in_specs=[VMEM] * 2,
        out_specs=VMEM,
        compiler_params=params(8),
        cost_estimate=cost(0),
        name="half",
    )(*args)


def local_kernel(res, q, k, v, done, km, kl, ka):
    def first(h):
        c = head_cols(h)
        qs = [q[block_rows(b), c] for b in range(BLOCKS)]
        scores = [[] for _ in range(BLOCKS)]
        for j in range(BLOCKS):
            users = qs[j : j + 2]
            s = dot_nt(jnp.concatenate(users, 0), k[block_rows(j), c]) * SCALE2
            for i in range(len(users)):
                scores[j + i].append(s[i * W0 : (i + 1) * W0])
        return scores

    def second(h, scores):
        c = head_cols(h)
        ms, ls, ps = [], [], []
        for b in range(BLOCKS):
            m = functools.reduce(
                jnp.maximum, [jnp.max(s, axis=1, keepdims=True) for s in scores[b]]
            )
            p = [jnp.exp2(s - m) for s in scores[b]]
            ms.append(m)
            ls.append(sum(jnp.sum(x, axis=1, keepdims=True) for x in p))
            ps.append([x.astype(BF16) for x in p])
        accs = [None] * BLOCKS
        for j in range(BLOCKS):
            users = [ps[j][-1]] + ([ps[j + 1][0]] if j + 1 < BLOCKS else [])
            o = dot(jnp.concatenate(users, 0), v[block_rows(j), c])
            for i in range(len(users)):
                part = o[i * W0 : (i + 1) * W0]
                accs[j + i] = part if accs[j + i] is None else accs[j + i] + part
        km[:W0, c], kl[:W0, c], ka[:W0, c] = wide(ms[0]), wide(ls[0]), accs[0]
        rest = []
        for b in range(1, BLOCKS):
            near = slice(OTHER + b * NEAR, OTHER + (b + 1) * NEAR)
            km[near, c] = wide(ms[b][OTHER:])
            kl[near, c] = wide(ls[b][OTHER:])
            ka[near, c] = accs[b][OTHER:]
            rest.append((accs[b][:OTHER] * (1.0 / ls[b][:OTHER])).astype(BF16))
        restore = res[block_rows(h), :OTHER]
        pair = dot(restore, jnp.concatenate(rest[:2], 1)).astype(BF16)
        done[0:W0, c] = pair[:, :DH]
        done[W0 : 2 * W0, c] = pair[:, DH:]
        done[2 * W0 :, c] = dot(restore, rest[2]).astype(BF16)

    staged(first, second)


def local(*args):
    state = out_of(KEPT, COLS, dtype=F32)
    return pl.pallas_call(
        local_kernel,
        out_shape=[
            out_of(TOK - W0, COLS),
            state,
            state,
            state,
        ],
        in_specs=[VMEM] * 4,
        out_specs=[VMEM] * 4,
        compiler_params=params(16),
        cost_estimate=cost(1),
        name="local",
    )(*args)


def halo_kernel(res, q, km, kl, ka, halo_c, halo, done, hm, hl, ha):
    position = lax.axis_index("seq")
    from_core = (position & 1) == 1
    has_halo = position > 0

    def first(h):
        c = head_cols(h)
        hk = jnp.where(from_core, halo_c[:, c], halo[:, c])
        return jnp.where(has_halo, dot_nt(q[:W0, c], hk) * SCALE2, -jnp.inf)

    def second(h, s):
        c, d = head_cols(h), value_cols(h)
        hv = jnp.where(from_core, halo_c[:, d], halo[:, d])
        m = km[:W0, c]
        m_new = jnp.maximum(m, wide(jnp.max(s, axis=1, keepdims=True)))
        p = jnp.exp2(s - jnp.concatenate([m_new, m_new], 1))
        scale = jnp.exp2(m - m_new)
        l = kl[:W0, c] * scale + wide(jnp.sum(p, axis=1, keepdims=True))
        acc = ka[:W0, c] * scale + dot(p.astype(BF16), hv)
        hm[:, c], hl[:, c], ha[:, c] = m_new[OTHER:], l[OTHER:], acc[OTHER:]
        rest = (acc[:OTHER] * (1.0 / l[:OTHER])).astype(BF16)
        done[:, c] = dot(res[block_rows(h), :OTHER], rest).astype(BF16)

    staged(first, second)


def halo_fold(*args):
    state = out_of(NEAR, COLS, dtype=F32)
    return pl.pallas_call(
        halo_kernel,
        out_shape=[out_of(W0, COLS), state, state, state],
        in_specs=[VMEM] * 7,
        out_specs=[VMEM] * 4,
        compiler_params=params(16),
        cost_estimate=cost(0),
        name="halo",
    )(*args)


def near_kernel(q, km, kl, ka, near, near_c, far_z, m, l, acc):
    def keys(cols):
        return jnp.concatenate([near[:, cols], near_c[:, cols], far_z[:, cols]], 0)

    def first(h):
        return dot_nt(q[:, head_cols(h)], keys(head_cols(h))) * SCALE2

    def second(h, s):
        c = head_cols(h)
        state = weigh(s, keys(value_cols(h)))
        later = merge([(km[W0:, c], kl[W0:, c], ka[W0:, c]), tuple(x[NEAR:] for x in state)])
        for ref, start, rest in zip((m, l, acc), state, later):
            ref[:NEAR, c] = start[:NEAR]
            ref[NEAR:, c] = rest

    staged(first, second)


def near(*args):
    return pl.pallas_call(
        near_kernel,
        out_shape=[out_of(NROWS, COLS, dtype=F32)] * 3,
        in_specs=[VMEM] * 7,
        out_specs=[VMEM] * 3,
        compiler_params=params(16),
        cost_estimate=cost(0),
        name="near",
    )(*args)


def across_kernel(q, nm, nl, na, given, other, rest_z, rest_zc, m, l, acc):
    core = lax.axis_index("seq") & 1

    def keys(h, start):
        half = slice(start // 2 + h % 2 * DH, start // 2 + (h % 2 + 1) * DH)
        cols = slice(start + h * DH, start + (h + 1) * DH)
        far = jnp.where(core == h // 2, given[:, half], other[:, half])
        return jnp.concatenate([far, rest_z[:, cols], rest_zc[:, cols]], 0)

    def first(h):
        return dot_nt(q[:, head_cols(h)], keys(h, 0)) * SCALE2

    def second(h, s):
        c = head_cols(h)
        m[:, c], l[:, c], acc[:, c] = merge(
            [(nm[:, c], nl[:, c], na[:, c]), weigh(s, keys(h, COLS))]
        )

    staged(first, second)


def across(*args):
    return pl.pallas_call(
        across_kernel,
        out_shape=[out_of(NROWS, COLS, dtype=F32)] * 3,
        in_specs=[VMEM] * 8,
        out_specs=[VMEM] * 3,
        compiler_params=params(16),
        cost_estimate=cost(0),
        name="across",
    )(*args)


def far_kernel(*refs):
    q, kv, out = refs[:4], refs[4:8], refs[8:]
    n = 2 * FROWS
    lane = lax.broadcasted_iota(jnp.int32, (4 * n, DH), 1)
    heads = range(HEADS // 2)
    scores = []
    for g in heads:
        c = head_cols(g)
        qh = jnp.concatenate([x[:, c] for x in q], 0)
        k = jnp.concatenate([x[:, c] for x in kv], 0)
        scores.append(dot_nt(qh, k) * SCALE2)
    tail = jnp.zeros((4 * n, DH), F32)
    for g in heads:
        c = head_cols(g)
        d = slice(HALF + g * DH, HALF + (g + 1) * DH)
        v = jnp.concatenate([x[:, d] for x in kv], 0)
        m = jnp.max(scores[g], axis=1, keepdims=True)
        p = jnp.exp2(scores[g] - m)
        l = wide(jnp.sum(p, axis=1, keepdims=True))
        o = (dot(p.astype(BF16), v) * (1.0 / l)).astype(BF16)
        left = wide(m) + jnp.log2(l)
        for e in range(3):
            piece = left.astype(BF16).astype(F32)
            tail = jnp.where(lane == 2 * e + g, piece, tail)
            left = left - piece
        for i, part in enumerate(out):
            part[:, c] = o[i * n : (i + 1) * n]
    tail = tail.astype(BF16)
    for i, part in enumerate(out):
        part[:, HALF:] = tail[i * n : (i + 1) * n]


def far(*args):
    return pl.pallas_call(
        far_kernel,
        out_shape=[out_of(2 * FROWS, SENT)] * 4,
        in_specs=[VMEM] * 8,
        out_specs=[VMEM] * 4,
        compiler_params=params(24),
        cost_estimate=cost(0),
        name="far",
    )(*args)


def fold_kernel(f0, f1, f2, f3, out):
    fars = (f0, f1, f2, f3)
    n = 2 * FROWS
    tails = jnp.concatenate([f[:, HALF:] for f in fars], 0)
    row = lax.broadcasted_iota(jnp.int32, (DH, DH), 0)
    for g in range(HEADS // 2):
        c = head_cols(g)
        gather = jnp.where((row < 6) & ((row & 1) == g), 1.0, 0.0).astype(BF16)
        lse = dot(tails, gather)
        states = [
            (lse[i * n : (i + 1) * n], 1.0, f[:, c].astype(F32)) for i, f in enumerate(fars)
        ]
        m, l, acc = merge(states)
        out[:, c] = acc * (1.0 / l)
        out[:, HALF + g * DH : HALF + (g + 1) * DH] = m + jnp.log2(l)


def fold(*args):
    return pl.pallas_call(
        fold_kernel,
        out_shape=out_of(2 * FROWS, COLS, dtype=F32),
        in_specs=[VMEM] * 4,
        out_specs=VMEM,
        compiler_params=params(8),
        cost_estimate=cost(0),
        name="fold",
    )(*args)


def join_kernel(
    far_z, res, hm, hl, ha, nm, nl, na, done0, done, mine, mine_c, out, block, sems
):
    core = lax.axis_index("seq") & 1
    restored = []
    for h in range(HEADS):
        c = head_cols(h)
        m, l, acc = nm[:, c], nl[:, c], na[:, c]
        g = h % 2
        fo, fm = (
            jnp.where(
                core == h // 2,
                jnp.where(core == 0, mine[:FROWS, cols], mine[FROWS:, cols]),
                jnp.where(core == 0, mine_c[:FROWS, cols], mine_c[FROWS:, cols]),
            )
            for cols in (head_cols(g), slice(HALF + g * DH, HALF + (g + 1) * DH))
        )
        for b in range(BLOCKS):
            rows = slice(b * NEAR, (b + 1) * NEAR)
            mb, lb, ab = m[rows], l[rows], acc[rows]
            if b == 0:
                mb, lb, ab = merge([(hm[:, c], hl[:, c], ha[:, c]), (mb, lb, ab)])
            fr = slice(b * FAR, (b + 1) * FAR)
            _, lf, af = merge([(mb[:FAR], lb[:FAR], ab[:FAR]), (fm[fr], 1.0, fo[fr])])
            restored.append(
                (
                    jnp.concatenate([af, ab[FAR:]], 0)
                    * (1.0 / jnp.concatenate([lf, lb[FAR:]], 0))
                ).astype(BF16)
            )
    copies = []
    for b in range(0, BLOCKS, 2):
        for h in range(HEADS):
            c = head_cols(h)
            pair = jnp.concatenate(restored[h * BLOCKS + b : h * BLOCKS + b + 2], 1)
            placed = dot(res[block_rows(h), OTHER:], pair).astype(BF16)
            for i in range(2):
                rest = done0[:, c] if b + i == 0 else done[block_rows(b + i - 1), c]
                block[block_rows(b + i), c] = rest + placed[:, i * DH : (i + 1) * DH]
        for i in range(2):
            rows = block_rows(b + i)
            copies.append(
                pltpu.make_async_copy(block.at[rows, :], out.at[rows, :], sems.at[b + i])
            )
            copies[-1].start()
    for copy in copies:
        copy.wait()


def join(*args):
    return pl.pallas_call(
        join_kernel,
        out_shape=out_of(TOK, COLS),
        in_specs=[VMEM] * 12,
        out_specs=HBM,
        scratch_shapes=[pltpu.VMEM((TOK, COLS), BF16), pltpu.SemaphoreType.DMA((BLOCKS,))],
        compiler_params=params(16),
        cost_estimate=cost(0),
        name="join",
    )(*args)


def place(x, y, z, core):
    return ((x % 4 * 4 + y % 4) * 2 + z % 2) * 2 + core


def moves(dx=0, dy=0, dz=0, dcore=0):
    return [
        (place(x, y, z, core), place(x + dx, y + dy, z + dz, (core + dcore) % 2))
        for x in range(4)
        for y in range(4)
        for z in range(2)
        for core in range(2)
    ]


def send(value, **shift):
    return lax.ppermute(value, "seq", moves(**shift))


def turn(value, step, keys):
    pairs = []
    for x in range(4):
        for y in range(4):
            for z in range(2):
                for core in range(2):
                    dx, dy = (step, 0) if (core == 0) == keys else (0, step)
                    pairs.append((place(x, y, z, core), place(x + dx, y + dy, z, core)))
    return lax.ppermute(value, "seq", pairs)


def shards(q, k, v, off):
    offs, kv_far, kv_rest, kv_near, halo = extract(off, k, v)
    far_z = send(kv_far, dz=1)
    near_c = send(kv_near, dcore=1)
    halo_c = send(halo, dcore=1)
    kv_rest, near_c = lax.optimization_barrier((kv_rest, near_c))
    rest_z = send(kv_rest, dz=1)
    qp, qn, q_keep, q_give, res = permute_queries(offs, q)
    q_give, halo_c = lax.optimization_barrier((q_give, halo_c))
    qm = pick_queries(q_keep, send(q_give, dcore=1))
    steps = (2, 1, -1)
    qs = [turn(qm, s, False) for s in steps]
    done, *kept = local(res, qp, k, v)
    far_z, *_ = lax.optimization_barrier((far_z, done, *qs))
    keep, give = split_far(far_z)
    given = send(give, dcore=1)
    own = pick_keys(kv_far, near_c, keep, given)
    gathered = [own] + [turn(own, s, True) for s in steps]
    halo, _ = lax.optimization_barrier((halo, own))
    halo = lax.ppermute(halo, "seq", [(s, s + 1) for s in range(1, 63, 2)])
    rest_z, *_ = lax.optimization_barrier((rest_z, *gathered, done))
    parts = far(qm, *qs, *gathered)
    rest_zc = send(rest_z, dcore=1)
    rest_zc, *parts = lax.optimization_barrier((rest_zc, *parts))
    keep, *_ = lax.optimization_barrier((keep, *parts))
    other = send(keep, dcore=1)
    back = [parts[0]] + [turn(p, -s, False) for p, s in zip(parts[1:], steps)]
    mine = fold(*back)
    state = near(qn, *kept, kv_near, near_c, far_z)
    state = across(qn, *state, given, other, rest_z, rest_zc)
    done0, *halo_state = halo_fold(res, qp, *kept, halo_c, halo)
    mine, *_ = lax.optimization_barrier((mine, halo, state[0]))
    mine_c = send(mine, dcore=1)
    return join(far_z, res, *halo_state, *state, done0, done, mine, mine_c)


def solution(mesh):
    placed = (P("seq", "head"), P("seq", "head"), P("seq", "head"), P("head"))
    return jax.shard_map(
        shards, mesh=mesh, in_specs=placed, out_specs=P("seq", "head"), check_vma=False
    )
```

```python
import functools

import jax
import jax.numpy as jnp
from jax import lax
from jax.experimental import pallas as pl
from jax.experimental.pallas import tpu as pltpu
from jax.sharding import PartitionSpec as P

HEADS = 4
DH = 128
W0 = 256
BLOCKS = 4
R1 = 4
R2 = 16
TOK = 1024
COLS = 512
NEAR = 64
FAR = 16
REST = NEAR - FAR
OTHER = W0 - NEAR
NROWS = NEAR * BLOCKS
FROWS = FAR * BLOCKS
KEPT = OTHER + NROWS
HALF = COLS // 2
SENT = HALF + DH
SCALE2 = 128**-0.5 * 1.4426950408889634
F32 = jnp.float32
BF16 = jnp.bfloat16

VMEM = pl.BlockSpec(memory_space=pltpu.VMEM)
HBM = pl.BlockSpec(memory_space=pltpu.HBM)


def out_of(*shape, dtype=BF16):
    return jax.ShapeDtypeStruct(shape, dtype)


def params(mib):
    return pltpu.CompilerParams(vmem_limit_bytes=mib << 20)


def cost(us):
    return pl.CostEstimate(flops=int(us * 1e9), bytes_accessed=1000, transcendentals=0)


def source_row(index, offset):
    order = index >> 4
    residue = ((order & 3) << 2) + (((order >> 2) + 1) & 3)
    return ((index & 15) << 4) + ((offset + residue) & 15)


def select_matrix(offset, start, count):
    index = lax.broadcasted_iota(jnp.int32, (count, W0), 0) + start
    row = lax.broadcasted_iota(jnp.int32, (count, W0), 1)
    return jnp.where(row == source_row(index, offset), 1.0, 0.0).astype(BF16)


def restore_matrix(offset, start, count):
    index = lax.broadcasted_iota(jnp.int32, (W0, count), 1) + start
    row = lax.broadcasted_iota(jnp.int32, (W0, count), 0)
    return jnp.where(row == source_row(index, offset), 1.0, 0.0).astype(BF16)


def dot(a, b):
    return jnp.dot(a, b, preferred_element_type=F32)


def dot_nt(a, b):
    return lax.dot_general(a, b, (((1,), (1,)), ((), ())), preferred_element_type=F32)


def wide(column):
    return jnp.broadcast_to(column, (column.shape[0], DH))


def staged(first, second):
    ready = first(0)
    for h in range(HEADS):
        later = first(h + 1) if h + 1 < HEADS else None
        second(h, ready)
        ready = later


def weigh(s, v):
    m = jnp.max(s, axis=1, keepdims=True)
    p = jnp.exp2(s - m)
    l = jnp.sum(p, axis=1, keepdims=True)
    return wide(m), wide(l), dot(p.astype(BF16), v)


def merge(states):
    m = functools.reduce(jnp.maximum, [s[0] for s in states])
    scales = [jnp.exp2(s[0] - m) for s in states]
    l = sum(s[1] * c for s, c in zip(states, scales))
    acc = sum(s[2] * c for s, c in zip(states, scales))
    return m, l, acc


def head_cols(h):
    return slice(h * DH, (h + 1) * DH)


def value_cols(h):
    return slice(COLS + h * DH, COLS + (h + 1) * DH)


def block_rows(b):
    return slice(b * W0, (b + 1) * W0)


def offset_rows(offs, h, width):
    row = offs[h : h + 1, :]
    return jnp.concatenate([row] * (width // DH), 1) if width > DH else row[:, :width]


def extract_kernel(
    off_hbm, k_hbm, v_hbm, offs, kv_far, kv_rest, kv_near, halo, off, k, v, k32, v32, off_sem, sems
):
    off_copy = pltpu.make_async_copy(off_hbm, off, off_sem)
    off_copy.start()
    copies = {}
    for b in reversed(range(BLOCKS)):
        for i, (src, dst) in enumerate(((k_hbm, k), (v_hbm, v))):
            copies[i, b] = pltpu.make_async_copy(
                src.at[block_rows(b), :], dst.at[block_rows(b), :], sems.at[i, b]
            )
            copies[i, b].start()
    off_copy.wait()
    for h in range(HEADS):
        offs[h : h + 1, :] = jnp.full((1, DH), off[h], jnp.int32)
    for b in reversed(range(BLOCKS)):
        rows = block_rows(b)
        for i, (src, dst) in enumerate(((k, k32), (v, v32))):
            copies[i, b].wait()
            if b == BLOCKS - 1:
                copies[i, BLOCKS] = pltpu.make_async_copy(
                    src.at[rows, :], halo.at[:, i * COLS : (i + 1) * COLS], sems.at[i, BLOCKS]
                )
                copies[i, BLOCKS].start()
            for h in range(HEADS):
                dst[h, rows, :] = src[rows, head_cols(h)].astype(F32)
    for h in range(HEADS):
        for a in range(R2 // R1):
            start = (off[h] + R1 * a) & (R2 - 1)
            for src, cols in ((k32, head_cols(h)), (v32, value_cols(h))):
                part = src[h, pl.ds(start, FROWS, stride=R2), :].astype(BF16)
                kv_near[a * FROWS : (a + 1) * FROWS, cols] = part
                if a == 0:
                    kv_far[:, cols] = part
                else:
                    kv_rest[(a - 1) * FROWS : a * FROWS, cols] = part
    for i in range(2):
        copies[i, BLOCKS].wait()


def extract(*args):
    return pl.pallas_call(
        extract_kernel,
        out_shape=[
            out_of(8, DH, dtype=jnp.int32),
            out_of(FROWS, 2 * COLS),
            out_of(REST * BLOCKS, 2 * COLS),
            out_of(NROWS, 2 * COLS),
            out_of(W0, 2 * COLS),
        ],
        in_specs=[HBM] * 3,
        out_specs=[VMEM] * 4 + [HBM],
        scratch_shapes=[
            pltpu.SMEM((HEADS,), jnp.int32),
            pltpu.VMEM((TOK, COLS), BF16),
            pltpu.VMEM((TOK, COLS), BF16),
            pltpu.VMEM((HEADS, TOK + R2, DH), F32),
            pltpu.VMEM((HEADS, TOK + R2, DH), F32),
            pltpu.SemaphoreType.DMA,
            pltpu.SemaphoreType.DMA((2, BLOCKS + 1)),
        ],
        compiler_params=params(59),
        cost_estimate=cost(0),
        name="extract",
    )(*args)


def queries_kernel(offs, q, qp, qn, q_keep, q_give, res):
    core = lax.axis_index("seq") & 1
    qf = {}
    sels = []
    for h in range(HEADS):
        offset = offset_rows(offs, h, W0)
        sels.append(select_matrix(offset, 0, W0))
        res[block_rows(h), :] = restore_matrix(offset, 0, W0)
    for b in range(0, BLOCKS, 2):
        for h in range(HEADS):
            c = head_cols(h)
            pair = jnp.concatenate([q[block_rows(b), c], q[block_rows(b + 1), c]], 1)
            moved = dot(sels[h], pair).astype(BF16)
            for i in range(2):
                part = moved[:, i * DH : (i + 1) * DH]
                qp[block_rows(b + i), c] = part
                qn[(b + i) * NEAR : (b + i + 1) * NEAR, c] = part[OTHER:]
                qf[b + i, h] = part[OTHER : OTHER + FAR]
    for b in range(BLOCKS):
        rows = slice(b * FAR, (b + 1) * FAR)
        for g in range(HEADS // 2):
            low, high = qf[b, g], qf[b, g + HEADS // 2]
            q_keep[rows, head_cols(g)] = jnp.where(core == 0, low, high)
            q_give[rows, head_cols(g)] = jnp.where(core == 0, high, low)


def permute_queries(*args):
    return pl.pallas_call(
        queries_kernel,
        out_shape=[
            out_of(TOK, COLS),
            out_of(NROWS, COLS),
            out_of(FROWS, HALF),
            out_of(FROWS, HALF),
            out_of(HEADS * W0, W0),
        ],
        in_specs=[VMEM] * 2,
        out_specs=[VMEM] * 5,
        compiler_params=params(16),
        cost_estimate=cost(12),
        name="queries",
    )(*args)


def pick(ref, core, start):
    return jnp.where(core == 0, ref[:, start : start + HALF], ref[:, start + HALF : start + COLS])


def split_kernel(far_z, keep, give):
    core = lax.axis_index("seq") & 1
    for start in (0, COLS):
        cols = slice(start // 2, start // 2 + HALF)
        keep[:, cols] = pick(far_z, core, start)
        give[:, cols] = pick(far_z, 1 - core, start)


def split_far(*args):
    return pl.pallas_call(
        split_kernel,
        out_shape=[out_of(FROWS, COLS)] * 2,
        in_specs=[VMEM],
        out_specs=[VMEM] * 2,
        compiler_params=params(8),
        cost_estimate=cost(0),
        name="split",
    )(*args)


def keys_kernel(kv_far, near_c, keep, given, own):
    core = lax.axis_index("seq") & 1
    for i, src in enumerate((kv_far, near_c.at[:FROWS, :])):
        rows = slice(i * FROWS, (i + 1) * FROWS)
        own[rows, :HALF] = pick(src, core, 0)
        own[rows, HALF:] = pick(src, core, COLS)
    own[2 * FROWS : 3 * FROWS, :] = keep[...]
    own[3 * FROWS :, :] = given[...]


def pick_keys(*args):
    return pl.pallas_call(
        keys_kernel,
        out_shape=out_of(4 * FROWS, COLS),
        in_specs=[VMEM] * 4,
        out_specs=VMEM,
        compiler_params=params(8),
        cost_estimate=cost(0),
        name="keys",
    )(*args)


def half_kernel(keep, given, out):
    core = lax.axis_index("seq") & 1
    out[:FROWS, :] = jnp.where(core == 0, keep[...], given[...])
    out[FROWS:, :] = jnp.where(core == 0, given[...], keep[...])


def pick_queries(*args):
    return pl.pallas_call(
        half_kernel,
        out_shape=out_of(2 * FROWS, HALF),
        in_specs=[VMEM] * 2,
        out_specs=VMEM,
        compiler_params=params(8),
        cost_estimate=cost(0),
        name="half",
    )(*args)


def local_kernel(res, q, k, v, done, km, kl, ka):
    def first(h):
        c = head_cols(h)
        qs = [q[block_rows(b), c] for b in range(BLOCKS)]
        scores = [[] for _ in range(BLOCKS)]
        for j in range(BLOCKS):
            users = qs[j : j + 2]
            s = dot_nt(jnp.concatenate(users, 0), k[block_rows(j), c]) * SCALE2
            for i in range(len(users)):
                scores[j + i].append(s[i * W0 : (i + 1) * W0])
        return scores

    def second(h, scores):
        c = head_cols(h)
        ms, ls, ps = [], [], []
        for b in range(BLOCKS):
            m = functools.reduce(
                jnp.maximum, [jnp.max(s, axis=1, keepdims=True) for s in scores[b]]
            )
            p = [jnp.exp2(s - m) for s in scores[b]]
            ms.append(m)
            ls.append(sum(jnp.sum(x, axis=1, keepdims=True) for x in p))
            ps.append([x.astype(BF16) for x in p])
        accs = [None] * BLOCKS
        for j in range(BLOCKS):
            users = [ps[j][-1]] + ([ps[j + 1][0]] if j + 1 < BLOCKS else [])
            o = dot(jnp.concatenate(users, 0), v[block_rows(j), c])
            for i in range(len(users)):
                part = o[i * W0 : (i + 1) * W0]
                accs[j + i] = part if accs[j + i] is None else accs[j + i] + part
        km[:W0, c], kl[:W0, c], ka[:W0, c] = wide(ms[0]), wide(ls[0]), accs[0]
        rest = []
        for b in range(1, BLOCKS):
            near = slice(OTHER + b * NEAR, OTHER + (b + 1) * NEAR)
            km[near, c] = wide(ms[b][OTHER:])
            kl[near, c] = wide(ls[b][OTHER:])
            ka[near, c] = accs[b][OTHER:]
            rest.append((accs[b][:OTHER] * (1.0 / ls[b][:OTHER])).astype(BF16))
        restore = res[block_rows(h), :OTHER]
        pair = dot(restore, jnp.concatenate(rest[:2], 1)).astype(BF16)
        done[0:W0, c] = pair[:, :DH]
        done[W0 : 2 * W0, c] = pair[:, DH:]
        done[2 * W0 :, c] = dot(restore, rest[2]).astype(BF16)

    staged(first, second)


def local(*args):
    state = out_of(KEPT, COLS, dtype=F32)
    return pl.pallas_call(
        local_kernel,
        out_shape=[
            out_of(TOK - W0, COLS),
            state,
            state,
            state,
        ],
        in_specs=[VMEM] * 4,
        out_specs=[VMEM] * 4,
        compiler_params=params(16),
        cost_estimate=cost(1),
        name="local",
    )(*args)


def halo_kernel(res, q, km, kl, ka, halo_c, halo, done, hm, hl, ha):
    position = lax.axis_index("seq")
    from_core = (position & 1) == 1
    has_halo = position > 0

    def first(h):
        c = head_cols(h)
        hk = jnp.where(from_core, halo_c[:, c], halo[:, c])
        return jnp.where(has_halo, dot_nt(q[:W0, c], hk) * SCALE2, -jnp.inf)

    def second(h, s):
        c, d = head_cols(h), value_cols(h)
        hv = jnp.where(from_core, halo_c[:, d], halo[:, d])
        m = km[:W0, c]
        m_new = jnp.maximum(m, wide(jnp.max(s, axis=1, keepdims=True)))
        p = jnp.exp2(s - jnp.concatenate([m_new, m_new], 1))
        scale = jnp.exp2(m - m_new)
        l = kl[:W0, c] * scale + wide(jnp.sum(p, axis=1, keepdims=True))
        acc = ka[:W0, c] * scale + dot(p.astype(BF16), hv)
        hm[:, c], hl[:, c], ha[:, c] = m_new[OTHER:], l[OTHER:], acc[OTHER:]
        rest = (acc[:OTHER] * (1.0 / l[:OTHER])).astype(BF16)
        done[:, c] = dot(res[block_rows(h), :OTHER], rest).astype(BF16)

    staged(first, second)


def halo_fold(*args):
    state = out_of(NEAR, COLS, dtype=F32)
    return pl.pallas_call(
        halo_kernel,
        out_shape=[out_of(W0, COLS), state, state, state],
        in_specs=[VMEM] * 7,
        out_specs=[VMEM] * 4,
        compiler_params=params(16),
        cost_estimate=cost(0),
        name="halo",
    )(*args)


def near_kernel(q, km, kl, ka, near, near_c, far_z, m, l, acc):
    def keys(cols):
        return jnp.concatenate([near[:, cols], near_c[:, cols], far_z[:, cols]], 0)

    def first(h):
        return dot_nt(q[:, head_cols(h)], keys(head_cols(h))) * SCALE2

    def second(h, s):
        c = head_cols(h)
        state = weigh(s, keys(value_cols(h)))
        later = merge([(km[W0:, c], kl[W0:, c], ka[W0:, c]), tuple(x[NEAR:] for x in state)])
        for ref, start, rest in zip((m, l, acc), state, later):
            ref[:NEAR, c] = start[:NEAR]
            ref[NEAR:, c] = rest

    staged(first, second)


def near(*args):
    return pl.pallas_call(
        near_kernel,
        out_shape=[out_of(NROWS, COLS, dtype=F32)] * 3,
        in_specs=[VMEM] * 7,
        out_specs=[VMEM] * 3,
        compiler_params=params(16),
        cost_estimate=cost(0),
        name="near",
    )(*args)


def across_kernel(q, nm, nl, na, given, other, rest_z, rest_zc, m, l, acc):
    core = lax.axis_index("seq") & 1

    def keys(h, start):
        half = slice(start // 2 + h % 2 * DH, start // 2 + (h % 2 + 1) * DH)
        cols = slice(start + h * DH, start + (h + 1) * DH)
        far = jnp.where(core == h // 2, given[:, half], other[:, half])
        return jnp.concatenate([far, rest_z[:, cols], rest_zc[:, cols]], 0)

    def first(h):
        return dot_nt(q[:, head_cols(h)], keys(h, 0)) * SCALE2

    def second(h, s):
        c = head_cols(h)
        m[:, c], l[:, c], acc[:, c] = merge(
            [(nm[:, c], nl[:, c], na[:, c]), weigh(s, keys(h, COLS))]
        )

    staged(first, second)


def across(*args):
    return pl.pallas_call(
        across_kernel,
        out_shape=[out_of(NROWS, COLS, dtype=F32)] * 3,
        in_specs=[VMEM] * 8,
        out_specs=[VMEM] * 3,
        compiler_params=params(16),
        cost_estimate=cost(0),
        name="across",
    )(*args)


def far_kernel(*refs):
    q, kv, out = refs[:4], refs[4:8], refs[8:]
    n = 2 * FROWS
    lane = lax.broadcasted_iota(jnp.int32, (4 * n, DH), 1)
    heads = range(HEADS // 2)
    scores = []
    for g in heads:
        c = head_cols(g)
        qh = jnp.concatenate([x[:, c] for x in q], 0)
        k = jnp.concatenate([x[:, c] for x in kv], 0)
        scores.append(dot_nt(qh, k) * SCALE2)
    tail = jnp.zeros((4 * n, DH), F32)
    for g in heads:
        c = head_cols(g)
        d = slice(HALF + g * DH, HALF + (g + 1) * DH)
        v = jnp.concatenate([x[:, d] for x in kv], 0)
        m = jnp.max(scores[g], axis=1, keepdims=True)
        p = jnp.exp2(scores[g] - m)
        l = wide(jnp.sum(p, axis=1, keepdims=True))
        o = (dot(p.astype(BF16), v) * (1.0 / l)).astype(BF16)
        left = wide(m) + jnp.log2(l)
        for e in range(3):
            piece = left.astype(BF16).astype(F32)
            tail = jnp.where(lane == 2 * e + g, piece, tail)
            left = left - piece
        for i, part in enumerate(out):
            part[:, c] = o[i * n : (i + 1) * n]
    tail = tail.astype(BF16)
    for i, part in enumerate(out):
        part[:, HALF:] = tail[i * n : (i + 1) * n]


def far(*args):
    return pl.pallas_call(
        far_kernel,
        out_shape=[out_of(2 * FROWS, SENT)] * 4,
        in_specs=[VMEM] * 8,
        out_specs=[VMEM] * 4,
        compiler_params=params(24),
        cost_estimate=cost(0),
        name="far",
    )(*args)


def fold_kernel(f0, f1, f2, f3, out):
    fars = (f0, f1, f2, f3)
    n = 2 * FROWS
    tails = jnp.concatenate([f[:, HALF:] for f in fars], 0)
    row = lax.broadcasted_iota(jnp.int32, (DH, DH), 0)
    for g in range(HEADS // 2):
        c = head_cols(g)
        gather = jnp.where((row < 6) & ((row & 1) == g), 1.0, 0.0).astype(BF16)
        lse = dot(tails, gather)
        states = [
            (lse[i * n : (i + 1) * n], 1.0, f[:, c].astype(F32)) for i, f in enumerate(fars)
        ]
        m, l, acc = merge(states)
        out[:, c] = acc * (1.0 / l)
        out[:, HALF + g * DH : HALF + (g + 1) * DH] = m + jnp.log2(l)


def fold(*args):
    return pl.pallas_call(
        fold_kernel,
        out_shape=out_of(2 * FROWS, COLS, dtype=F32),
        in_specs=[VMEM] * 4,
        out_specs=VMEM,
        compiler_params=params(8),
        cost_estimate=cost(0),
        name="fold",
    )(*args)


def join_kernel(
    far_z, res, hm, hl, ha, nm, nl, na, done0, done, mine, mine_c, out, block, sems
):
    core = lax.axis_index("seq") & 1
    restored = []
    for h in range(HEADS):
        c = head_cols(h)
        m, l, acc = nm[:, c], nl[:, c], na[:, c]
        g = h % 2
        fo, fm = (
            jnp.where(
                core == h // 2,
                jnp.where(core == 0, mine[:FROWS, cols], mine[FROWS:, cols]),
                jnp.where(core == 0, mine_c[:FROWS, cols], mine_c[FROWS:, cols]),
            )
            for cols in (head_cols(g), slice(HALF + g * DH, HALF + (g + 1) * DH))
        )
        for b in range(BLOCKS):
            rows = slice(b * NEAR, (b + 1) * NEAR)
            mb, lb, ab = m[rows], l[rows], acc[rows]
            if b == 0:
                mb, lb, ab = merge([(hm[:, c], hl[:, c], ha[:, c]), (mb, lb, ab)])
            fr = slice(b * FAR, (b + 1) * FAR)
            _, lf, af = merge([(mb[:FAR], lb[:FAR], ab[:FAR]), (fm[fr], 1.0, fo[fr])])
            restored.append(
                (
                    jnp.concatenate([af, ab[FAR:]], 0)
                    * (1.0 / jnp.concatenate([lf, lb[FAR:]], 0))
                ).astype(BF16)
            )
    copies = []
    for b in range(0, BLOCKS, 2):
        for h in range(HEADS):
            c = head_cols(h)
            pair = jnp.concatenate(restored[h * BLOCKS + b : h * BLOCKS + b + 2], 1)
            placed = dot(res[block_rows(h), OTHER:], pair).astype(BF16)
            for i in range(2):
                rest = done0[:, c] if b + i == 0 else done[block_rows(b + i - 1), c]
                block[block_rows(b + i), c] = rest + placed[:, i * DH : (i + 1) * DH]
        for i in range(2):
            rows = block_rows(b + i)
            copies.append(
                pltpu.make_async_copy(block.at[rows, :], out.at[rows, :], sems.at[b + i])
            )
            copies[-1].start()
    for copy in copies:
        copy.wait()


def join(*args):
    return pl.pallas_call(
        join_kernel,
        out_shape=out_of(TOK, COLS),
        in_specs=[VMEM] * 12,
        out_specs=HBM,
        scratch_shapes=[pltpu.VMEM((TOK, COLS), BF16), pltpu.SemaphoreType.DMA((BLOCKS,))],
        compiler_params=params(16),
        cost_estimate=cost(0),
        name="join",
    )(*args)


def place(x, y, z, core):
    return ((x % 4 * 4 + y % 4) * 2 + z % 2) * 2 + core


def moves(dx=0, dy=0, dz=0, dcore=0):
    return [
        (place(x, y, z, core), place(x + dx, y + dy, z + dz, (core + dcore) % 2))
        for x in range(4)
        for y in range(4)
        for z in range(2)
        for core in range(2)
    ]


def send(value, **shift):
    return lax.ppermute(value, "seq", moves(**shift))


def turn(value, step, keys):
    pairs = []
    for x in range(4):
        for y in range(4):
            for z in range(2):
                for core in range(2):
                    dx, dy = (step, 0) if (core == 0) == keys else (0, step)
                    pairs.append((place(x, y, z, core), place(x + dx, y + dy, z, core)))
    return lax.ppermute(value, "seq", pairs)


def shards(q, k, v, off):
    offs, kv_far, kv_rest, kv_near, halo = extract(off, k, v)
    far_z = send(kv_far, dz=1)
    near_c = send(kv_near, dcore=1)
    halo_c = send(halo, dcore=1)
    kv_rest, near_c = lax.optimization_barrier((kv_rest, near_c))
    rest_z = send(kv_rest, dz=1)
    qp, qn, q_keep, q_give, res = permute_queries(offs, q)
    q_give, halo_c = lax.optimization_barrier((q_give, halo_c))
    qm = pick_queries(q_keep, send(q_give, dcore=1))
    steps = (2, 1, -1)
    qs = [turn(qm, s, False) for s in steps]
    done, *kept = local(res, qp, k, v)
    far_z, *_ = lax.optimization_barrier((far_z, done, *qs))
    keep, give = split_far(far_z)
    given = send(give, dcore=1)
    own = pick_keys(kv_far, near_c, keep, given)
    gathered = [own] + [turn(own, s, True) for s in steps]
    halo, _ = lax.optimization_barrier((halo, own))
    halo = lax.ppermute(halo, "seq", [(s, s + 1) for s in range(1, 63, 2)])
    rest_z, *_ = lax.optimization_barrier((rest_z, *gathered, done))
    parts = far(qm, *qs, *gathered)
    rest_zc = send(rest_z, dcore=1)
    rest_zc, *parts = lax.optimization_barrier((rest_zc, *parts))
    keep, *_ = lax.optimization_barrier((keep, *parts))
    other = send(keep, dcore=1)
    back = [parts[0]] + [turn(p, -s, False) for p, s in zip(parts[1:], steps)]
    mine = fold(*back)
    state = near(qn, *kept, kv_near, near_c, far_z)
    state = across(qn, *state, given, other, rest_z, rest_zc)
    done0, *halo_state = halo_fold(res, qp, *kept, halo_c, halo)
    mine, *_ = lax.optimization_barrier((mine, halo, state[0]))
    mine_c = send(mine, dcore=1)
    return join(far_z, res, *halo_state, *state, done0, done, mine, mine_c)


def solution(mesh):
    placed = (P("seq", "head"), P("seq", "head"), P("seq", "head"), P("head"))
    return jax.shard_map(
        shards, mesh=mesh, in_specs=placed, out_specs=P("seq", "head"), check_vma=False
    )
```

```python
import functools

import jax
import jax.numpy as jnp
from jax import lax
from jax.experimental import pallas as pl
from jax.experimental.pallas import tpu as pltpu
from jax.sharding import PartitionSpec as P

HEADS = 4
DH = 128
W0 = 256
BLOCKS = 4
R1 = 4
R2 = 16
TOK = 1024
COLS = 512
NEAR = 64
FAR = 16
REST = NEAR - FAR
OTHER = W0 - NEAR
NROWS = NEAR * BLOCKS
FROWS = FAR * BLOCKS
KEPT = OTHER + NROWS
HALF = COLS // 2
SENT = HALF + DH
SCALE2 = 128**-0.5 * 1.4426950408889634
F32 = jnp.float32
BF16 = jnp.bfloat16

VMEM = pl.BlockSpec(memory_space=pltpu.VMEM)
HBM = pl.BlockSpec(memory_space=pltpu.HBM)


def out_of(*shape, dtype=BF16):
    return jax.ShapeDtypeStruct(shape, dtype)


def params(mib):
    return pltpu.CompilerParams(vmem_limit_bytes=mib << 20)


def cost(us):
    return pl.CostEstimate(flops=int(us * 1e9), bytes_accessed=1000, transcendentals=0)


def source_row(index, offset):
    order = index >> 4
    residue = ((order & 3) << 2) + (((order >> 2) + 1) & 3)
    return ((index & 15) << 4) + ((offset + residue) & 15)


def select_matrix(offset, start, count):
    index = lax.broadcasted_iota(jnp.int32, (count, W0), 0) + start
    row = lax.broadcasted_iota(jnp.int32, (count, W0), 1)
    return jnp.where(row == source_row(index, offset), 1.0, 0.0).astype(BF16)


def restore_matrix(offset, start, count):
    index = lax.broadcasted_iota(jnp.int32, (W0, count), 1) + start
    row = lax.broadcasted_iota(jnp.int32, (W0, count), 0)
    return jnp.where(row == source_row(index, offset), 1.0, 0.0).astype(BF16)


def dot(a, b):
    return jnp.dot(a, b, preferred_element_type=F32)


def dot_nt(a, b):
    return lax.dot_general(a, b, (((1,), (1,)), ((), ())), preferred_element_type=F32)


def wide(column):
    return jnp.broadcast_to(column, (column.shape[0], DH))


def staged(first, second):
    ready = first(0)
    for h in range(HEADS):
        later = first(h + 1) if h + 1 < HEADS else None
        second(h, ready)
        ready = later


def weigh(s, v):
    m = jnp.max(s, axis=1, keepdims=True)
    p = jnp.exp2(s - m)
    l = jnp.sum(p, axis=1, keepdims=True)
    return wide(m), wide(l), dot(p.astype(BF16), v)


def merge(states):
    m = functools.reduce(jnp.maximum, [s[0] for s in states])
    scales = [jnp.exp2(s[0] - m) for s in states]
    l = sum(s[1] * c for s, c in zip(states, scales))
    acc = sum(s[2] * c for s, c in zip(states, scales))
    return m, l, acc


def head_cols(h):
    return slice(h * DH, (h + 1) * DH)


def value_cols(h):
    return slice(COLS + h * DH, COLS + (h + 1) * DH)


def block_rows(b):
    return slice(b * W0, (b + 1) * W0)


def offset_rows(offs, h, width):
    row = offs[h : h + 1, :]
    return jnp.concatenate([row] * (width // DH), 1) if width > DH else row[:, :width]


def extract_kernel(
    off_hbm, k_hbm, v_hbm, offs, kv_far, kv_rest, kv_near, halo, off, k, v, k32, v32, off_sem, sems
):
    off_copy = pltpu.make_async_copy(off_hbm, off, off_sem)
    off_copy.start()
    copies = {}
    for b in reversed(range(BLOCKS)):
        for i, (src, dst) in enumerate(((k_hbm, k), (v_hbm, v))):
            copies[i, b] = pltpu.make_async_copy(
                src.at[block_rows(b), :], dst.at[block_rows(b), :], sems.at[i, b]
            )
            copies[i, b].start()
    off_copy.wait()
    for h in range(HEADS):
        offs[h : h + 1, :] = jnp.full((1, DH), off[h], jnp.int32)
    for b in reversed(range(BLOCKS)):
        rows = block_rows(b)
        for i, (src, dst) in enumerate(((k, k32), (v, v32))):
            copies[i, b].wait()
            if b == BLOCKS - 1:
                copies[i, BLOCKS] = pltpu.make_async_copy(
                    src.at[rows, :], halo.at[:, i * COLS : (i + 1) * COLS], sems.at[i, BLOCKS]
                )
                copies[i, BLOCKS].start()
            for h in range(HEADS):
                dst[h, rows, :] = src[rows, head_cols(h)].astype(F32)
    for h in range(HEADS):
        for a in range(R2 // R1):
            start = (off[h] + R1 * a) & (R2 - 1)
            for src, cols in ((k32, head_cols(h)), (v32, value_cols(h))):
                part = src[h, pl.ds(start, FROWS, stride=R2), :].astype(BF16)
                kv_near[a * FROWS : (a + 1) * FROWS, cols] = part
                if a == 0:
                    kv_far[:, cols] = part
                else:
                    kv_rest[(a - 1) * FROWS : a * FROWS, cols] = part
    for i in range(2):
        copies[i, BLOCKS].wait()


def extract(*args):
    return pl.pallas_call(
        extract_kernel,
        out_shape=[
            out_of(8, DH, dtype=jnp.int32),
            out_of(FROWS, 2 * COLS),
            out_of(REST * BLOCKS, 2 * COLS),
            out_of(NROWS, 2 * COLS),
            out_of(W0, 2 * COLS),
        ],
        in_specs=[HBM] * 3,
        out_specs=[VMEM] * 4 + [HBM],
        scratch_shapes=[
            pltpu.SMEM((HEADS,), jnp.int32),
            pltpu.VMEM((TOK, COLS), BF16),
            pltpu.VMEM((TOK, COLS), BF16),
            pltpu.VMEM((HEADS, TOK + R2, DH), F32),
            pltpu.VMEM((HEADS, TOK + R2, DH), F32),
            pltpu.SemaphoreType.DMA,
            pltpu.SemaphoreType.DMA((2, BLOCKS + 1)),
        ],
        compiler_params=params(59),
        cost_estimate=cost(0),
        name="extract",
    )(*args)


def queries_kernel(offs, q_hbm, qp, qn, q_keep, q_give, res, q, sems):
    core = lax.axis_index("seq") & 1
    qf = {}
    copies = []
    for b in range(BLOCKS):
        copies.append(
            pltpu.make_async_copy(q_hbm.at[block_rows(b), :], q.at[block_rows(b), :], sems.at[b])
        )
        copies[-1].start()
    sels = []
    for h in range(HEADS):
        offset = offset_rows(offs, h, W0)
        sels.append(select_matrix(offset, 0, W0))
        res[block_rows(h), :] = restore_matrix(offset, 0, W0)
    for b in range(0, BLOCKS, 2):
        copies[b].wait()
        copies[b + 1].wait()
        for h in range(HEADS):
            c = head_cols(h)
            pair = jnp.concatenate([q[block_rows(b), c], q[block_rows(b + 1), c]], 1)
            moved = dot(sels[h], pair).astype(BF16)
            for i in range(2):
                part = moved[:, i * DH : (i + 1) * DH]
                qp[block_rows(b + i), c] = part
                qn[(b + i) * NEAR : (b + i + 1) * NEAR, c] = part[OTHER:]
                qf[b + i, h] = part[OTHER : OTHER + FAR]
    for b in range(BLOCKS):
        rows = slice(b * FAR, (b + 1) * FAR)
        for g in range(HEADS // 2):
            low, high = qf[b, g], qf[b, g + HEADS // 2]
            q_keep[rows, head_cols(g)] = jnp.where(core == 0, low, high)
            q_give[rows, head_cols(g)] = jnp.where(core == 0, high, low)


def permute_queries(*args):
    return pl.pallas_call(
        queries_kernel,
        out_shape=[
            out_of(TOK, COLS),
            out_of(NROWS, COLS),
            out_of(FROWS, HALF),
            out_of(FROWS, HALF),
            out_of(HEADS * W0, W0),
        ],
        in_specs=[VMEM, HBM],
        out_specs=[VMEM] * 5,
        scratch_shapes=[pltpu.VMEM((TOK, COLS), BF16), pltpu.SemaphoreType.DMA((BLOCKS,))],
        compiler_params=params(58),
        cost_estimate=cost(12),
        name="queries",
    )(*args)


def pick(ref, core, start):
    return jnp.where(core == 0, ref[:, start : start + HALF], ref[:, start + HALF : start + COLS])


def split_kernel(far_z, keep, give):
    core = lax.axis_index("seq") & 1
    for start in (0, COLS):
        cols = slice(start // 2, start // 2 + HALF)
        keep[:, cols] = pick(far_z, core, start)
        give[:, cols] = pick(far_z, 1 - core, start)


def split_far(*args):
    return pl.pallas_call(
        split_kernel,
        out_shape=[out_of(FROWS, COLS)] * 2,
        in_specs=[VMEM],
        out_specs=[VMEM] * 2,
        compiler_params=params(8),
        cost_estimate=cost(0),
        name="split",
    )(*args)


def keys_kernel(kv_far, near_c, keep, given, own):
    core = lax.axis_index("seq") & 1
    for i, src in enumerate((kv_far, near_c.at[:FROWS, :])):
        rows = slice(i * FROWS, (i + 1) * FROWS)
        own[rows, :HALF] = pick(src, core, 0)
        own[rows, HALF:] = pick(src, core, COLS)
    own[2 * FROWS : 3 * FROWS, :] = keep[...]
    own[3 * FROWS :, :] = given[...]


def pick_keys(*args):
    return pl.pallas_call(
        keys_kernel,
        out_shape=out_of(4 * FROWS, COLS),
        in_specs=[VMEM] * 4,
        out_specs=VMEM,
        compiler_params=params(8),
        cost_estimate=cost(0),
        name="keys",
    )(*args)


def half_kernel(keep, given, out):
    core = lax.axis_index("seq") & 1
    out[:FROWS, :] = jnp.where(core == 0, keep[...], given[...])
    out[FROWS:, :] = jnp.where(core == 0, given[...], keep[...])


def pick_queries(*args):
    return pl.pallas_call(
        half_kernel,
        out_shape=out_of(2 * FROWS, HALF),
        in_specs=[VMEM] * 2,
        out_specs=VMEM,
        compiler_params=params(8),
        cost_estimate=cost(0),
        name="half",
    )(*args)


def local_kernel(res, q, k, v, done, km, kl, ka):
    def first(h):
        c = head_cols(h)
        qs = [q[block_rows(b), c] for b in range(BLOCKS)]
        scores = [[] for _ in range(BLOCKS)]
        for j in range(BLOCKS):
            users = qs[j : j + 2]
            s = dot_nt(jnp.concatenate(users, 0), k[block_rows(j), c]) * SCALE2
            for i in range(len(users)):
                scores[j + i].append(s[i * W0 : (i + 1) * W0])
        return scores

    def second(h, scores):
        c = head_cols(h)
        ms, ls, ps = [], [], []
        for b in range(BLOCKS):
            m = functools.reduce(
                jnp.maximum, [jnp.max(s, axis=1, keepdims=True) for s in scores[b]]
            )
            p = [jnp.exp2(s - m) for s in scores[b]]
            ms.append(m)
            ls.append(sum(jnp.sum(x, axis=1, keepdims=True) for x in p))
            ps.append([x.astype(BF16) for x in p])
        accs = [None] * BLOCKS
        for j in range(BLOCKS):
            users = [ps[j][-1]] + ([ps[j + 1][0]] if j + 1 < BLOCKS else [])
            o = dot(jnp.concatenate(users, 0), v[block_rows(j), c])
            for i in range(len(users)):
                part = o[i * W0 : (i + 1) * W0]
                accs[j + i] = part if accs[j + i] is None else accs[j + i] + part
        km[:W0, c], kl[:W0, c], ka[:W0, c] = wide(ms[0]), wide(ls[0]), accs[0]
        rest = []
        for b in range(1, BLOCKS):
            near = slice(OTHER + b * NEAR, OTHER + (b + 1) * NEAR)
            km[near, c] = wide(ms[b][OTHER:])
            kl[near, c] = wide(ls[b][OTHER:])
            ka[near, c] = accs[b][OTHER:]
            rest.append((accs[b][:OTHER] * (1.0 / ls[b][:OTHER])).astype(BF16))
        restore = res[block_rows(h), :OTHER]
        pair = dot(restore, jnp.concatenate(rest[:2], 1)).astype(BF16)
        done[0:W0, c] = pair[:, :DH]
        done[W0 : 2 * W0, c] = pair[:, DH:]
        done[2 * W0 :, c] = dot(restore, rest[2]).astype(BF16)

    staged(first, second)


def local(*args):
    state = out_of(KEPT, COLS, dtype=F32)
    return pl.pallas_call(
        local_kernel,
        out_shape=[
            out_of(TOK - W0, COLS),
            state,
            state,
            state,
        ],
        in_specs=[VMEM] * 4,
        out_specs=[VMEM] * 4,
        compiler_params=params(16),
        cost_estimate=cost(1),
        name="local",
    )(*args)


def halo_kernel(res, q, km, kl, ka, halo_c, halo, done, hm, hl, ha):
    position = lax.axis_index("seq")
    from_core = (position & 1) == 1
    has_halo = position > 0

    def first(h):
        c = head_cols(h)
        hk = jnp.where(from_core, halo_c[:, c], halo[:, c])
        return jnp.where(has_halo, dot_nt(q[:W0, c], hk) * SCALE2, -jnp.inf)

    def second(h, s):
        c, d = head_cols(h), value_cols(h)
        hv = jnp.where(from_core, halo_c[:, d], halo[:, d])
        m = km[:W0, c]
        m_new = jnp.maximum(m, wide(jnp.max(s, axis=1, keepdims=True)))
        p = jnp.exp2(s - jnp.concatenate([m_new, m_new], 1))
        scale = jnp.exp2(m - m_new)
        l = kl[:W0, c] * scale + wide(jnp.sum(p, axis=1, keepdims=True))
        acc = ka[:W0, c] * scale + dot(p.astype(BF16), hv)
        hm[:, c], hl[:, c], ha[:, c] = m_new[OTHER:], l[OTHER:], acc[OTHER:]
        rest = (acc[:OTHER] * (1.0 / l[:OTHER])).astype(BF16)
        done[:, c] = dot(res[block_rows(h), :OTHER], rest).astype(BF16)

    staged(first, second)


def halo_fold(*args):
    state = out_of(NEAR, COLS, dtype=F32)
    return pl.pallas_call(
        halo_kernel,
        out_shape=[out_of(W0, COLS), state, state, state],
        in_specs=[VMEM] * 7,
        out_specs=[VMEM] * 4,
        compiler_params=params(16),
        cost_estimate=cost(0),
        name="halo",
    )(*args)


def near_kernel(q, km, kl, ka, near, near_c, far_z, m, l, acc):
    def keys(cols):
        return jnp.concatenate([near[:, cols], near_c[:, cols], far_z[:, cols]], 0)

    def first(h):
        return dot_nt(q[:, head_cols(h)], keys(head_cols(h))) * SCALE2

    def second(h, s):
        c = head_cols(h)
        state = weigh(s, keys(value_cols(h)))
        later = merge([(km[W0:, c], kl[W0:, c], ka[W0:, c]), tuple(x[NEAR:] for x in state)])
        for ref, start, rest in zip((m, l, acc), state, later):
            ref[:NEAR, c] = start[:NEAR]
            ref[NEAR:, c] = rest

    staged(first, second)


def near(*args):
    return pl.pallas_call(
        near_kernel,
        out_shape=[out_of(NROWS, COLS, dtype=F32)] * 3,
        in_specs=[VMEM] * 7,
        out_specs=[VMEM] * 3,
        compiler_params=params(16),
        cost_estimate=cost(0),
        name="near",
    )(*args)


def across_kernel(q, nm, nl, na, given, other, rest_z, rest_zc, m, l, acc):
    core = lax.axis_index("seq") & 1

    def keys(h, start):
        half = slice(start // 2 + h % 2 * DH, start // 2 + (h % 2 + 1) * DH)
        cols = slice(start + h * DH, start + (h + 1) * DH)
        far = jnp.where(core == h // 2, given[:, half], other[:, half])
        return jnp.concatenate([far, rest_z[:, cols], rest_zc[:, cols]], 0)

    def first(h):
        return dot_nt(q[:, head_cols(h)], keys(h, 0)) * SCALE2

    def second(h, s):
        c = head_cols(h)
        m[:, c], l[:, c], acc[:, c] = merge(
            [(nm[:, c], nl[:, c], na[:, c]), weigh(s, keys(h, COLS))]
        )

    staged(first, second)


def across(*args):
    return pl.pallas_call(
        across_kernel,
        out_shape=[out_of(NROWS, COLS, dtype=F32)] * 3,
        in_specs=[VMEM] * 8,
        out_specs=[VMEM] * 3,
        compiler_params=params(16),
        cost_estimate=cost(0),
        name="across",
    )(*args)


def far_kernel(*refs):
    q, kv, out = refs[:4], refs[4:8], refs[8:]
    n = 2 * FROWS
    lane = lax.broadcasted_iota(jnp.int32, (4 * n, DH), 1)
    heads = range(HEADS // 2)
    scores = []
    for g in heads:
        c = head_cols(g)
        qh = jnp.concatenate([x[:, c] for x in q], 0)
        k = jnp.concatenate([x[:, c] for x in kv], 0)
        scores.append(dot_nt(qh, k) * SCALE2)
    tail = jnp.zeros((4 * n, DH), F32)
    for g in heads:
        c = head_cols(g)
        d = slice(HALF + g * DH, HALF + (g + 1) * DH)
        v = jnp.concatenate([x[:, d] for x in kv], 0)
        m = jnp.max(scores[g], axis=1, keepdims=True)
        p = jnp.exp2(scores[g] - m)
        l = wide(jnp.sum(p, axis=1, keepdims=True))
        o = (dot(p.astype(BF16), v) * (1.0 / l)).astype(BF16)
        left = wide(m) + jnp.log2(l)
        for e in range(3):
            piece = left.astype(BF16).astype(F32)
            tail = jnp.where(lane == 2 * e + g, piece, tail)
            left = left - piece
        for i, part in enumerate(out):
            part[:, c] = o[i * n : (i + 1) * n]
    tail = tail.astype(BF16)
    for i, part in enumerate(out):
        part[:, HALF:] = tail[i * n : (i + 1) * n]


def far(*args):
    return pl.pallas_call(
        far_kernel,
        out_shape=[out_of(2 * FROWS, SENT)] * 4,
        in_specs=[VMEM] * 8,
        out_specs=[VMEM] * 4,
        compiler_params=params(24),
        cost_estimate=cost(0),
        name="far",
    )(*args)


def fold_kernel(f0, f1, f2, f3, out):
    fars = (f0, f1, f2, f3)
    n = 2 * FROWS
    tails = jnp.concatenate([f[:, HALF:] for f in fars], 0)
    row = lax.broadcasted_iota(jnp.int32, (DH, DH), 0)
    for g in range(HEADS // 2):
        c = head_cols(g)
        gather = jnp.where((row < 6) & ((row & 1) == g), 1.0, 0.0).astype(BF16)
        lse = dot(tails, gather)
        states = [
            (lse[i * n : (i + 1) * n], 1.0, f[:, c].astype(F32)) for i, f in enumerate(fars)
        ]
        m, l, acc = merge(states)
        out[:, c] = acc * (1.0 / l)
        out[:, HALF + g * DH : HALF + (g + 1) * DH] = m + jnp.log2(l)


def fold(*args):
    return pl.pallas_call(
        fold_kernel,
        out_shape=out_of(2 * FROWS, COLS, dtype=F32),
        in_specs=[VMEM] * 4,
        out_specs=VMEM,
        compiler_params=params(8),
        cost_estimate=cost(0),
        name="fold",
    )(*args)


def join_kernel(
    far_z, res, hm, hl, ha, nm, nl, na, done0, done, mine, mine_c, out, block, sems
):
    core = lax.axis_index("seq") & 1
    restored = []
    for h in range(HEADS):
        c = head_cols(h)
        m, l, acc = nm[:, c], nl[:, c], na[:, c]
        g = h % 2
        fo, fm = (
            jnp.where(
                core == h // 2,
                jnp.where(core == 0, mine[:FROWS, cols], mine[FROWS:, cols]),
                jnp.where(core == 0, mine_c[:FROWS, cols], mine_c[FROWS:, cols]),
            )
            for cols in (head_cols(g), slice(HALF + g * DH, HALF + (g + 1) * DH))
        )
        for b in range(BLOCKS):
            rows = slice(b * NEAR, (b + 1) * NEAR)
            mb, lb, ab = m[rows], l[rows], acc[rows]
            if b == 0:
                mb, lb, ab = merge([(hm[:, c], hl[:, c], ha[:, c]), (mb, lb, ab)])
            fr = slice(b * FAR, (b + 1) * FAR)
            _, lf, af = merge([(mb[:FAR], lb[:FAR], ab[:FAR]), (fm[fr], 1.0, fo[fr])])
            restored.append(
                (
                    jnp.concatenate([af, ab[FAR:]], 0)
                    * (1.0 / jnp.concatenate([lf, lb[FAR:]], 0))
                ).astype(BF16)
            )
    copies = []
    for b in range(0, BLOCKS, 2):
        for h in range(HEADS):
            c = head_cols(h)
            pair = jnp.concatenate(restored[h * BLOCKS + b : h * BLOCKS + b + 2], 1)
            placed = dot(res[block_rows(h), OTHER:], pair).astype(BF16)
            for i in range(2):
                rest = done0[:, c] if b + i == 0 else done[block_rows(b + i - 1), c]
                block[block_rows(b + i), c] = rest + placed[:, i * DH : (i + 1) * DH]
        for i in range(2):
            rows = block_rows(b + i)
            copies.append(
                pltpu.make_async_copy(block.at[rows, :], out.at[rows, :], sems.at[b + i])
            )
            copies[-1].start()
    for copy in copies:
        copy.wait()


def join(*args):
    return pl.pallas_call(
        join_kernel,
        out_shape=out_of(TOK, COLS),
        in_specs=[VMEM] * 12,
        out_specs=HBM,
        scratch_shapes=[pltpu.VMEM((TOK, COLS), BF16), pltpu.SemaphoreType.DMA((BLOCKS,))],
        compiler_params=params(16),
        cost_estimate=cost(0),
        name="join",
    )(*args)


def place(x, y, z, core):
    return ((x % 4 * 4 + y % 4) * 2 + z % 2) * 2 + core


def moves(dx=0, dy=0, dz=0, dcore=0):
    return [
        (place(x, y, z, core), place(x + dx, y + dy, z + dz, (core + dcore) % 2))
        for x in range(4)
        for y in range(4)
        for z in range(2)
        for core in range(2)
    ]


def send(value, **shift):
    return lax.ppermute(value, "seq", moves(**shift))


def turn(value, step, keys):
    pairs = []
    for x in range(4):
        for y in range(4):
            for z in range(2):
                for core in range(2):
                    dx, dy = (step, 0) if (core == 0) == keys else (0, step)
                    pairs.append((place(x, y, z, core), place(x + dx, y + dy, z, core)))
    return lax.ppermute(value, "seq", pairs)


def shards(q, k, v, off):
    offs, kv_far, kv_rest, kv_near, halo = extract(off, k, v)
    far_z = send(kv_far, dz=1)
    near_c = send(kv_near, dcore=1)
    halo_c = send(halo, dcore=1)
    kv_rest, near_c = lax.optimization_barrier((kv_rest, near_c))
    rest_z = send(kv_rest, dz=1)
    qp, qn, q_keep, q_give, res = permute_queries(offs, q)
    q_give, halo_c = lax.optimization_barrier((q_give, halo_c))
    qm = pick_queries(q_keep, send(q_give, dcore=1))
    steps = (2, 1, -1)
    qs = [turn(qm, s, False) for s in steps]
    done, *kept = local(res, qp, k, v)
    far_z, *_ = lax.optimization_barrier((far_z, done, *qs))
    keep, give = split_far(far_z)
    given = send(give, dcore=1)
    own = pick_keys(kv_far, near_c, keep, given)
    gathered = [own] + [turn(own, s, True) for s in steps]
    halo, _ = lax.optimization_barrier((halo, own))
    halo = lax.ppermute(halo, "seq", [(s, s + 1) for s in range(1, 63, 2)])
    rest_z, *_ = lax.optimization_barrier((rest_z, *gathered, done))
    parts = far(qm, *qs, *gathered)
    rest_zc = send(rest_z, dcore=1)
    rest_zc, *parts = lax.optimization_barrier((rest_zc, *parts))
    keep, *_ = lax.optimization_barrier((keep, *parts))
    other = send(keep, dcore=1)
    back = [parts[0]] + [turn(p, -s, False) for p, s in zip(parts[1:], steps)]
    mine = fold(*back)
    state = near(qn, *kept, kv_near, near_c, far_z)
    state = across(qn, *state, given, other, rest_z, rest_zc)
    done0, *halo_state = halo_fold(res, qp, *kept, halo_c, halo)
    mine, *_ = lax.optimization_barrier((mine, halo, state[0]))
    mine_c = send(mine, dcore=1)
    return join(far_z, res, *halo_state, *state, done0, done, mine, mine_c)


def solution(mesh):
    placed = (P("seq", "head"), P("seq", "head"), P("seq", "head"), P("head"))
    return jax.shard_map(
        shards, mesh=mesh, in_specs=placed, out_specs=P("seq", "head"), check_vma=False
    )
```
